32 devices in a mesh: dp: 8 (over y, x, core), mp: 4 (over z).
Axes of the slice: x: 2, y: 2, z: 4, core: 2. Of those that a mesh axis runs over, the one named last changes fastest.
Arguments:
- bytes_in: bfloat16 [32, 2048, 768], P('dp', 'mp'), may hold values from -6 to 6
- mask_ratio: int32 [32], P('dp'), may hold values from 5 to 39
- mask_starts: int32 [32, 3], P('dp'), may hold values from 0 to 2047
- mask_lengths: int32 [32, 3], P('dp'), may hold values from 1 to 512
- latents: bfloat16 [256, 1280], P('mp', 'dp'), may hold values from -6 to 6
- col: bfloat16 [6, 1280, 1280], P(None, 'dp', 'mp'), may hold values from -0.15625 to 0.15625
- attn_out: bfloat16 [2, 1280, 1280], P(None, 'dp', 'mp'), may hold values from -1.25 to 1.25
- mlp_down: bfloat16 [2, 1280, 1280], P(None, 'dp', 'mp'), may hold values from -0.15625 to 0.15625
- enc_kv: bfloat16 [2, 768, 1280], P(None, 'dp', 'mp'), may hold values from -0.21875 to 0.21875
- dec_kv: bfloat16 [2, 1280, 768], P(None, 'dp', 'mp'), may hold values from -0.15625 to 0.15625
- dec_queries: bfloat16 [2048, 768], P('mp', 'dp'), may hold values from -6 to 6
- dec_square: bfloat16 [2, 768, 768], P(None, ('dp', 'mp')), may hold values from -0.21875 to 0.21875
- vocab: bfloat16 [768, 262], P(('dp', 'mp')), may hold values from -1.75 to 1.75
- gains: bfloat16 [5, 1280], P(None, ('dp', 'mp')), may hold values from 0.5 to 1.5
- mask_vec: bfloat16 [768], P(('dp', 'mp')), may hold values from -6 to 6
- byte_gain: bfloat16 [768], P(('dp', 'mp')), may hold values from 0.5 to 1.5
- cotangent: bfloat16 [32, 2048, 262], P('dp', 'mp'), may hold values from -6 to 6
Outputs:
- logits: bfloat16 [32, 2048, 262], P('dp', 'mp')
- bytes_grad: float32 [32, 2048, 768], P('dp', 'mp')
- latents_grad: float32 [256, 1280], P('mp', 'dp')
- col_grad: float32 [6, 1280, 1280], P(None, 'dp', 'mp')
- attn_out_grad: float32 [2, 1280, 1280], P(None, 'dp', 'mp')
- mlp_down_grad: float32 [2, 1280, 1280], P(None, 'dp', 'mp')
- enc_kv_grad: float32 [2, 768, 1280], P(None, 'dp', 'mp')
- dec_kv_grad: float32 [2, 1280, 768], P(None, 'dp', 'mp')
- dec_queries_grad: float32 [2048, 768], P('mp', 'dp')
- dec_square_grad: float32 [2, 768, 768], P(None, ('dp', 'mp'))
- vocab_grad: float32 [768, 262], P(('dp', 'mp'))
- gains_grad: float32 [5, 1280], P(None, ('dp', 'mp'))
- mask_vec_grad: float32 [768], P(('dp', 'mp'))
- byte_gain_grad: float32 [768], P(('dp', 'mp'))
The draws below stay inside these ranges and needn't reach their ends.
Inputs may be any that keep to these rules, and one draw needn't show every extreme that they name: `mask_starts`: spans may run past the last byte; only bytes inside the item are masked. Spans may intersect. `mask_ratio`: percent of positions masked by the spaced pattern.
All inputs are finite; a program needn't handle non-finite values.
Results may differ from the reference program's by a relative error of at most 0.035.
Values may be sent and summed in bfloat16 or wider, within the bound.
No kernel may reach another device: no remote copies, remote signals or barrier semaphores. Data moves between devices by JAX's collectives and lax.ppermute only.
A program may use at most 320 MiB of HBM per device.

```python
import jax
import jax.numpy as jnp
from jax import lax

D = 768
C = 1280
NLAT = 256
HEADS = 8
V = 262
HEAD = 160
SEQ = 2048
SPANS = 3
ITEMS = 32


def set_ends(drawn, rng, least, largest):
    index_at = [jax.random.randint(jax.random.fold_in(rng, axis), (), 0, length) for axis, length in enumerate(drawn.shape)]
    longest = drawn.shape.index(max(drawn.shape))
    beside = index_at[:longest] + [(index_at[longest] + 1) % drawn.shape[longest]] + index_at[longest + 1:]
    return drawn.at[tuple(index_at)].set(least).at[tuple(beside)].set(largest)


def steps_of(own_key, extent, shards, low, top_value):
    def one(position, parts):
        draws = jax.random.uniform(jax.random.fold_in(jax.random.fold_in(own_key, 6), position), (parts,), jnp.float32, low / len(shards), top_value / len(shards))
        return jnp.repeat(jnp.exp(draws), extent[position] // parts).reshape((-1,) + (1,) * (len(extent) - position - 1))

    level = one(*shards[0])
    for cut in shards[1:]:
        level = level * one(*cut)
    return level


def noise(own_key, shape, scale, limit, split=(), held_as=jnp.bfloat16):
    level = steps_of(own_key, shape, split, -0.22, 0.18) if split else 1.0
    drawn = jax.random.normal(own_key, shape, jnp.float32) * scale * level
    return jnp.minimum(jnp.maximum(drawn, -limit), limit).astype(held_as)


def setup_inputs(seed: int = 0) -> dict:
    seeds = jax.random.split(jax.random.key(seed), 18)
    bytes_in = noise(seeds[0], (ITEMS, SEQ, D), 1.0, 6.0, ((0, 8), (1, 4)))
    mask_ratio = set_ends(jax.random.randint(seeds[1], (ITEMS,), 5, 40), jax.random.fold_in(seeds[1], 1), 5, 39).astype(jnp.int32)
    mask_starts = set_ends(jax.random.randint(seeds[2], (ITEMS, SPANS), 0, SEQ), jax.random.fold_in(seeds[2], 1), 0, SEQ - 1).astype(jnp.int32)
    mask_lengths = set_ends(jax.random.randint(seeds[3], (ITEMS, SPANS), 1, SEQ // 4 + 1), jax.random.fold_in(seeds[3], 1), 1, (SEQ // 4 + 1) - 1).astype(jnp.int32)
    latents = noise(seeds[4], (NLAT, C), 1.0, 6.0, ((0, 4), (1, 8)))
    col = noise(seeds[5], (6, C, C), C ** -0.5, 0.15625, ((1, 8), (2, 4)))
    attn_out = noise(seeds[6], (2, C, C), (C // 64) ** -0.5, 1.25, ((1, 8), (2, 4)))
    mlp_down = noise(seeds[7], (2, C, C), C ** -0.5, 0.15625, ((1, 8), (2, 4)))
    enc_kv = noise(seeds[8], (2, D, C), D ** -0.5, 0.21875, ((1, 8), (2, 4)))
    dec_kv = noise(seeds[9], (2, C, D), C ** -0.5, 0.15625, ((1, 8), (2, 4)))
    dec_queries = noise(seeds[10], (SEQ, D), 1.0, 6.0, ((0, 4), (1, 8)))
    dec_square = noise(seeds[11], (2, D, D), D ** -0.5, 0.21875, ((1, 32),))
    vocab = noise(seeds[12], (D, V), (D // 64) ** -0.5, 1.75, ((0, 32),))
    gains = jnp.clip(1.0 + 0.1 * jax.random.normal(seeds[13], (5, C), jnp.float32), 0.5, 1.5).astype(jnp.bfloat16)
    mask_vec = noise(seeds[14], (D,), 1.0, 6.0, ((0, 32),))
    byte_gain = jnp.clip(1.0 + 0.1 * jax.random.normal(seeds[15], (D,), jnp.float32), 0.5, 1.5).astype(jnp.bfloat16)
    cotangent = noise(seeds[16], (ITEMS, SEQ, V), 1.0, 6.0, ((0, 8), (1, 4)))
    return {"bytes_in": bytes_in, "mask_ratio": mask_ratio, "mask_starts": mask_starts, "mask_lengths": mask_lengths, "latents": latents, "col": col, "attn_out": attn_out, "mlp_down": mlp_down, "enc_kv": enc_kv, "dec_kv": dec_kv, "dec_queries": dec_queries, "dec_square": dec_square, "vocab": vocab, "gains": gains, "mask_vec": mask_vec, "byte_gain": byte_gain, "cotangent": cotangent}


@jax.custom_vjp
def low(v):
    return lax.optimization_barrier(v.astype(jnp.bfloat16)).astype(jnp.float32)

@jax.custom_vjp
def low_back(v):
    return v

def low_keep(v):
    return (low(v), None)

def low_pass(kept, grad):
    return (grad,)

def back_keep(v):
    return (v, None)

def back_low(kept, grad):
    return (low(grad),)
low.defvjp(low_keep, low_pass)
low_back.defvjp(back_keep, back_low)

def matmul(left, right):
    return jnp.dot(left, right, precision=lax.Precision.HIGHEST)

def matmul_t(left, right):
    return lax.dot_general(left, right, (((left.ndim - 1,), (right.ndim - 1,)), ((), ())), precision=lax.Precision.HIGHEST)

def layer_norm(value, gain):
    centre = value - lax.optimization_barrier(jnp.mean(value, -1, keepdims=True))
    spread = lax.optimization_barrier(jnp.mean(centre * centre, -1, keepdims=True))
    return centre * lax.rsqrt(spread + 1e-05) * gain

def softmax_rows(scores):
    top = lax.optimization_barrier(jnp.max(scores, -1, keepdims=True))
    weights = jnp.exp(scores - top)
    return weights / lax.optimization_barrier(jnp.sum(weights, -1, keepdims=True))

def masked_rows(ratio, starts, lengths, positions):
    spaced = positions * 73 % 100 < ratio
    within = (positions[:, None] >= starts[None, :]) & (positions[:, None] < starts[None, :] + lengths[None, :])
    return jnp.where(spaced | jnp.any(within, axis=1), 1.0, 0.0).astype(jnp.float32)[:, None]

def feed_forward(resid, gain, w_up, w_down):
    normed = low(layer_norm(resid, gain))
    hidden = low_back(matmul(normed, w_up))
    return low_back(matmul_t(low(jax.nn.gelu(hidden, approximate=False)), w_down))

def self_attention(resid, gain, w_query, w_key, w_value, w_out):
    normed = low(layer_norm(resid, gain))
    query = low_back(low(matmul(normed, w_query) * HEAD ** (-0.5))).reshape(NLAT, HEADS, HEAD)
    keys = low_back(low(matmul(normed, w_key))).reshape(NLAT, HEADS, HEAD)
    values = low_back(low(matmul(normed, w_value))).reshape(NLAT, HEADS, HEAD)
    scores = low_back(jnp.einsum('qhe,khe->hqk', query, keys, precision=lax.Precision.HIGHEST))
    probs = low(softmax_rows(scores))
    mixed = jnp.einsum('hqk,khe->qhe', probs, values, precision=lax.Precision.HIGHEST)
    mixed = low_back(low(mixed)).reshape(NLAT, C)
    return low_back(matmul_t(mixed, w_out))

def item_forward(params, item):
    latents, col, attn_out, mlp_down, enc_kv, dec_kv, dec_queries, dec_square, vocab, gains, mask_vec, byte_gain = params
    bytes_row, masked = item
    start = bytes_row + masked * (mask_vec - bytes_row)
    byte_norm = low(layer_norm(start, byte_gain))
    lat_norm = low(layer_norm(latents, gains[0]))
    query = low_back(low(matmul(lat_norm, col[0]) * C ** (-0.5)))
    keys = low_back(low(matmul(byte_norm, enc_kv[0])))
    values = low_back(low(matmul(byte_norm, enc_kv[1])))
    scores = low_back(matmul_t(query, keys))
    probs = low(softmax_rows(scores))
    attended = low_back(low(matmul(probs, values)))
    first = latents + low_back(matmul_t(attended, attn_out[0]))
    second = first + feed_forward(first, gains[1], col[1], mlp_down[0])
    third = second + self_attention(second, gains[2], col[2], col[3], col[4], attn_out[1])
    fourth = third + feed_forward(third, gains[3], col[5], mlp_down[1])
    key_norm = low(layer_norm(fourth, gains[4]))
    dec_keys = low_back(low(matmul(key_norm, dec_kv[0])))
    dec_values = low_back(low(matmul(key_norm, dec_kv[1])))
    dec_query = low_back(low(matmul(dec_queries, dec_square[0]) * D ** (-0.5)))
    dec_scores = low_back(matmul_t(dec_query, dec_keys))
    dec_probs = low(softmax_rows(dec_scores))
    dec_mixed = low_back(low(matmul(dec_probs, dec_values)))
    decoded = low_back(low(matmul(dec_mixed, dec_square[1])))
    return matmul(decoded, vocab)

def reference(bytes_in, mask_ratio, mask_starts, mask_lengths, latents, col, attn_out, mlp_down, enc_kv, dec_kv, dec_queries, dec_square, vocab, gains, mask_vec, byte_gain, cotangent):
    params = tuple((w.astype(jnp.float32) for w in (latents, col, attn_out, mlp_down, enc_kv, dec_kv, dec_queries, dec_square, vocab, gains, mask_vec, byte_gain)))
    positions = jnp.arange(SEQ, dtype=jnp.int32)
    masks = jax.vmap(lambda ratio, starts, lengths: masked_rows(ratio, starts, lengths, positions))(mask_ratio, mask_starts, mask_lengths)
    inputs = bytes_in.astype(jnp.float32)
    step = jax.checkpoint(item_forward)

    def run(weights, items):

        def scan_body(carry, item):
            return (carry, step(weights, item))
        _, outputs = lax.scan(scan_body, jnp.zeros((), jnp.float32), (items, masks))
        return outputs
    logits, pullback = jax.vjp(run, params, inputs)
    grads, bytes_grad = pullback(cotangent.astype(jnp.float32) * masks)
    return (logits.astype(jnp.bfloat16), bytes_grad, grads[0], grads[1], grads[2], grads[3], grads[4], grads[5], grads[6], grads[7], grads[8], grads[9], grads[10], grads[11])
```

```python
import functools
import math

import jax
import jax.numpy as jnp
from jax import lax
from jax.sharding import PartitionSpec as P

HEAD = 160
BF = jnp.bfloat16
F32 = jnp.float32


def dot(left, right):
    return jnp.dot(left, right, preferred_element_type=F32)


def dot_t(left, right):
    return lax.dot_general(
        left,
        right,
        (((left.ndim - 1,), (right.ndim - 1,)), ((), ())),
        preferred_element_type=F32,
    )


def dot_tn(left, right):
    return lax.dot_general(left, right, (((0,), (0,)), ((), ())), preferred_element_type=F32)


def layer_norm(value, gain):
    centre = value - jnp.mean(value, -1, keepdims=True)
    spread_sq = jnp.mean(centre * centre, -1, keepdims=True)
    return centre * lax.rsqrt(spread_sq + 1e-05) * gain


def norm_back(value, gain, grad):
    centre = value - jnp.mean(value, -1, keepdims=True)
    inv = lax.rsqrt(jnp.mean(centre * centre, -1, keepdims=True) + 1e-05)
    unit = centre * inv
    scaled = grad * gain
    d_value = inv * (
        scaled
        - jnp.mean(scaled, -1, keepdims=True)
        - unit * jnp.mean(scaled * unit, -1, keepdims=True)
    )
    return d_value, grad * unit


def masked_rows(ratio, starts, lengths, positions):
    spaced = positions * 73 % 100 < ratio
    within = (positions[:, None] >= starts[None, :]) & (
        positions[:, None] < starts[None, :] + lengths[None, :]
    )
    return jnp.where(spaced | jnp.any(within, axis=1), 1.0, 0.0).astype(F32)


def gelu_exact(value):
    return jax.nn.gelu(value, approximate=False)


def gelu_slope(value):
    return 0.5 * (1.0 + lax.erf(value * 0.7071067811865476)) + value * 0.3989422804014327 * jnp.exp(
        -0.5 * value * value
    )


def nothing_of(value):
    return value[0, 0].astype(F32) * 0.0


class Links:
    def __init__(self, dn, mn):
        self.dn, self.mn = dn, mn
        self.bits = dn.bit_length() - 1
        assert 1 << self.bits == dn and mn & (mn - 1) == 0
        self.chips = [1 << b for b in range(1, self.bits)]
        self.d = lax.axis_index("dp")
        self.z = lax.axis_index("mp")

    def z_of(self, t):
        return (self.z - t) % self.mn

    def ring(self, value):
        parts = [value]
        for _ in range(self.mn - 1):
            parts += yield [("z", 1, parts[-1])]
        return parts

    def direct(self, values):
        got = yield [("z", t, values[t]) for t in range(1, self.mn)]
        return [values[0]] + list(got)

    def natural_z(self, parts):
        shape = parts[0].shape
        size = math.prod(shape[:-1])
        around = [parts[(-k) % self.mn].reshape(size, shape[-1]) for k in range(self.mn)] * 2
        first = ((self.mn - self.z) % self.mn) * size
        whole = lax.dynamic_slice_in_dim(jnp.concatenate(around, 0), first, self.mn * size, 0)
        return [whole[k * size : (k + 1) * size].reshape(shape) for k in range(self.mn)]

    def natural_rows(self, parts):
        size = parts[0].shape[0]
        around = jnp.concatenate([parts[(-k) % self.mn] for k in range(self.mn)] * 2, 0)
        return lax.dynamic_slice_in_dim(
            around, ((self.mn - self.z) % self.mn) * size, self.mn * size, 0
        )

    def natural_columns(self, parts):
        size = parts[0].shape[1]
        around = jnp.concatenate([parts[(-k) % self.mn] for k in range(self.mn)] * 2, 1)
        return lax.dynamic_slice_in_dim(
            around, ((self.mn - self.z) % self.mn) * size, self.mn * size, 1
        )

    def free(self, steps):
        got = None
        while True:
            try:
                sends = steps.send(got)
            except StopIteration as end:
                return end.value
            got = [self.send(*send) for send in sends]

    def send(self, lane, move, value):
        if lane == "z":
            pairs = [(i, (i + move) % self.mn) for i in range(self.mn)]
            return lax.ppermute(value, "mp", pairs)
        return lax.ppermute(value, "dp", [(i, i ^ lane) for i in range(self.dn)])

    def by_index(self, value):
        value = value.reshape((2,) * self.bits + value.shape[1:])
        for axis in range(self.bits):
            up = (self.d >> (self.bits - 1 - axis)) & 1
            value = jnp.where(up == 1, jnp.flip(value, axis), value)
        return value.reshape((self.dn,) + value.shape[self.bits :])

    def spread(self, piece, turned):
        pieces = {0: piece}
        ready = []
        for bit in turned:
            for key in list(pieces):
                mates, ready = ready, []
                got = yield [(bit, 0, pieces[key])] + [(1, 0, pieces[k]) for k in mates]
                pieces[key ^ bit] = got[0]
                pieces.update({k ^ 1: v for k, v in zip(mates, got[1:])})
                ready = [key ^ bit] + ([0] if key == 0 and bit == turned[0] else [])
        got = yield [(1, 0, pieces[k]) for k in ready]
        pieces.update({k ^ 1: v for k, v in zip(ready, got)})
        return pieces

    def sum_ring(self, block):
        total = block(1).astype(BF)
        for t in range(2, self.mn):
            (got,) = yield [("z", 1, total)]
            total = (got.astype(F32) + block(t).astype(F32)).astype(BF)
        (got,) = yield [("z", 1, total)]
        return got.astype(F32) + block(0).astype(F32)

    def sum_mp(self, value):
        got = yield from self.direct([value] * self.mn)
        return sum(self.natural_z(got))

    def sum_mp_rows(self, value):
        size = value.shape[0] // self.mn
        parts = [
            lax.dynamic_slice_in_dim(value, ((self.z + t) % self.mn) * size, size, 0).astype(BF)
            for t in range(self.mn)
        ]
        got = yield from self.direct(parts)
        total = sum(part.astype(F32) for part in got).astype(BF)
        got = yield from self.direct([total] * self.mn)
        return self.natural_rows(got)

    def sum_all(self, value):
        for bit in [1] + self.chips:
            (got,) = yield [(bit, 0, value)]
            value = value + got
        return (yield from self.sum_mp(value))

    def sum_all_rows(self, value):
        for b in range(self.bits):
            half = value.shape[0] // 2
            low, high = value[:half], value[half:]
            up = (self.d >> b) & 1
            give = jnp.where(up == 1, low, high).astype(BF)
            (got,) = yield [(1 << b, 0, give)]
            value = jnp.where(up == 1, high, low) + got.astype(F32)
        value = value.astype(BF)
        value = yield from self.direct([value] * self.mn)
        size = value[0].shape[0]
        value = self.natural_rows(value).astype(F32)
        value = sum(value[k * size : (k + 1) * size] for k in range(self.mn)).astype(BF)
        for b in reversed(range(self.bits)):
            (other,) = yield [(1 << b, 0, value)]
            up = (self.d >> b) & 1
            value = jnp.concatenate(
                [jnp.where(up == 1, other, value), jnp.where(up == 1, value, other)], 0
            )
        return value


def heads_of(value):
    return value.reshape(value.shape[0], -1, HEAD)


def per_device(
    dn,
    mn,
    bytes_in,
    mask_ratio,
    mask_starts,
    mask_lengths,
    latents,
    col,
    attn_out,
    mlp_down,
    enc_kv,
    dec_kv,
    dec_queries,
    dec_square,
    vocab,
    gains,
    mask_vec,
    byte_gain,
    cotangent,
):
    links = Links(dn, mn)
    d, z = links.d, links.z
    items, rows, wide_in = bytes_in.shape
    repeat = mn // items
    assert repeat * items == mn
    seq = rows * mn
    mine = z % items
    chan = col.shape[1] * dn
    enc_scale = chan ** (-0.5)
    dec_scale = wide_in ** (-0.5)

    n_gain, own_gain = gains.shape
    own_in = mask_vec.shape[0]
    in_rows = enc_kv.shape[1]
    col_rows, col_wide = col.shape[1:]
    own_lat, lat_cols = latents.shape
    small = jnp.concatenate([gains.reshape(-1), mask_vec, byte_gain])
    n_small = small.shape[0]
    line = jnp.pad(small, (0, -n_small % lat_cols)).reshape(-1, lat_cols)
    line = jnp.pad(line, ((0, -line.shape[0] % max(16 // mn, 1)), (0, 0)))
    chips = links.chips

    def head_task():
        early = yield from links.direct([jnp.concatenate([latents, line], 0)] * mn)
        early = links.natural_z(early)
        lat = [part[:own_lat] for part in early]
        tall = jnp.concatenate([part[own_lat:] for part in early] + lat, 0)
        n_line = tall.shape[0] - own_lat * mn
        heavy = jnp.concatenate([col[0], enc_kv[0]], 0)
        heavy = jnp.pad(heavy, ((n_line, own_lat * mn - heavy.shape[0]), (0, 0)))
        return (yield from links.spread(jnp.concatenate([tall, heavy], 1), chips))

    cat = lambda parts: jnp.concatenate(parts, -1)

    own_sq = dec_square.shape[1]
    n_voc = vocab.shape[1]
    deck_wide = dec_kv.shape[2]
    own_query, own_pos = dec_queries.T.shape

    def gathered(parts, wide):
        parts = [jnp.pad(p, ((0, -p.shape[0] % 16), (0, wide - p.shape[1]))) for p in parts]
        whole = jnp.concatenate(parts, 0)
        tall = whole.shape[0]
        whole = lax.all_gather(whole, ("dp", "mp"), axis=0, tiled=True)
        whole = whole.reshape(dn, mn, tall, wide)
        edges = [0]
        for p in parts:
            edges.append(edges[-1] + p.shape[0])
        return whole, edges

    def beside(got, row, col, size, wide):
        parts = [got[:, m, row : row + size, col : col + wide] for m in range(mn)]
        return jnp.concatenate([part.reshape(dn * size, wide) for part in parts], 1)

    side = lambda *parts: jnp.concatenate(parts, 1)
    w_one, at_one = gathered(
        [
            side(attn_out[0], col[1]),
            side(mlp_down[0], col[2]),
            side(col[3], col[4]),
            side(attn_out[1], jnp.pad(enc_kv[1], ((0, col_rows - in_rows), (0, 0)))),
        ],
        2 * col_wide,
    )
    late_wide = 2 * (col_wide + deck_wide)
    sq = side(dec_square[0], dec_square[1], vocab)
    sq = jnp.pad(sq, ((0, -own_sq % 16), (0, -sq.shape[1] % late_wide)))
    halves = 2 if own_query % 32 == 0 and 2 * own_pos <= late_wide else 1
    part_rows = own_query // halves
    def first_weight(k):
        return beside(w_one, at_one[k // 2], (k % 2) * col_wide, col_rows, col_wide)

    def last_weights():
        edge = 0
        out = []
        for wide in (col_wide, col_wide, deck_wide, deck_wide):
            out.append(beside(w_two, 0, edge, col_rows, wide))
            edge += wide
        query = [
            w_two[:, :, at_two[1] : at_two[1] + part_rows, h * own_pos : (h + 1) * own_pos]
            for h in range(halves)
        ]
        query = jnp.stack(query, 1).transpose(0, 1, 3, 2, 4).reshape(dn * own_query, seq)
        lines = jnp.concatenate(
            [w_two[:, :, row : row + own_sq] for row in at_two[2:-1]], -1
        ).reshape(dn * mn * own_sq, -1)
        return out + [
            query,
            lines[:, :wide_in],
            lines[:, wide_in : 2 * wide_in],
            lines[:, 2 * wide_in : 2 * wide_in + n_voc],
        ]

    steps = jnp.arange(rows, dtype=jnp.int32)
    masked = jax.vmap(lambda a, b, c: masked_rows(a, b, c, z * rows + steps))(
        mask_ratio, mask_starts, mask_lengths
    )[:, :, None]
    masked_item = masked_rows(
        mask_ratio[mine], mask_starts[mine], mask_lengths[mine], jnp.arange(seq, dtype=jnp.int32)
    )
    cot = cotangent.swapaxes(1, 2)
    head = links.free(head_task())
    held = links.by_index(jnp.stack([head[r] for r in range(dn)]))

    late_parts = [
        side(col[5], mlp_down[1], dec_kv[0], dec_kv[1]),
        jnp.concatenate(jnp.split(dec_queries.T, halves, 0), 1),
    ] + jnp.split(sq, sq.shape[1] // late_wide, 1)
    n_lat = own_lat * mn
    n_line = line.shape[0] * mn
    smalls = held[:, :n_line, :lat_cols].reshape(dn, mn, -1)[:, :, :n_small].astype(F32)
    gain = smalls[:, :, : n_gain * own_gain].reshape(dn, mn, n_gain, own_gain)
    gain = gain.transpose(2, 0, 1, 3).reshape(n_gain, -1)
    vecs = smalls[:, :, n_gain * own_gain :]
    mask_all = vecs[:, :, :own_in].reshape(-1)
    byte_gain_all = vecs[:, :, own_in:].reshape(-1)
    lat = held[:, n_line:, :lat_cols].transpose(1, 0, 2).reshape(n_lat, -1).astype(F32)
    col_zero = held[:, n_line : n_line + col_rows, lat_cols:].reshape(dn * col_rows, -1)
    key_w = held[:, n_line + col_rows : n_line + col_rows + in_rows, lat_cols:]
    key_w = key_w.reshape(dn * in_rows, -1)
    lat_norm = layer_norm(lat, gain[0]).astype(BF)
    query_m = (dot(lat_norm, col_zero) * enc_scale).astype(BF)
    query_key = dot_t(query_m, key_w)
    query_key = links.free(links.sum_mp_rows(query_key))

    raw = bytes_in.astype(F32)
    start = raw + masked * (mask_all - raw)
    byte_norm = layer_norm(start, byte_gain_all).astype(BF)

    scores = jnp.einsum("ld,ird->ilr", query_key, byte_norm, preferred_element_type=F32)
    top = jnp.max(scores, -1)
    weights = jnp.exp(scores - top[:, :, None])
    below = jnp.sum(weights, -1)
    mix = jnp.einsum("ilr,ird->ild", weights.astype(BF), byte_norm, preferred_element_type=F32)
    mix = mix.astype(BF)

    def mix_task(mix, top, below):
        block = lambda t: lax.dynamic_index_in_dim(mix, links.z_of(t) % items, 0, False)
        pack = jnp.stack([top, below])
        got = yield [("z", t, pack) for t in range(1, mn)] + [("z", 1, block(1))]
        stats = jnp.stack([pack] + list(got[: mn - 1]))
        top_all = jnp.max(stats[:, 0], 0)
        shares = jnp.exp(stats[:, 0] - top_all)
        total = sum(links.natural_z(list(stats[:, 1] * shares)))
        pick = lambda t, i: lax.dynamic_index_in_dim(shares[t], i % items, 0, False)[:, None]
        arrived = got[-1].astype(F32) * pick(1 % mn, links.z_of(2))
        for t in range(2, mn):
            arrived = (arrived + block(t).astype(F32) * pick(0, links.z_of(t))).astype(BF)
            (arrived,) = yield [("z", 1, arrived)]
            arrived = arrived.astype(F32)
        whole = arrived + block(0).astype(F32) * pick(0, z)
        whole = whole / lax.dynamic_index_in_dim(total, mine, 0, False)[:, None]
        return whole.astype(BF), shares[0] / total

    assert mn > 2
    mix, share = links.free(mix_task(mix, top, below))
    def cot_task():
        parts = [lax.dynamic_index_in_dim(cot, (z + t) % mn % items, 0, False) for t in range(mn)]
        parts = yield from links.direct(parts)
        return (links.natural_columns(parts).astype(F32) * (masked_item / repeat)[None, :]).astype(BF)

    w_out0, w_up0, w_down0, w_q, w_k, w_v, w_out1 = (first_weight(k) for k in range(7))
    w_value = beside(w_one, at_one[3], col_wide, in_rows, col_wide)
    late_parts[0] = late_parts[0] + (nothing_of(w_one[0, 0]) + nothing_of(mix)).astype(BF)
    w_two, at_two = gathered(
        late_parts,
        late_wide,
    )


    attended = dot(mix, w_value).astype(BF)
    first = lat + dot_t(attended, w_out0)
    norm1 = layer_norm(first, gain[1]).astype(BF)
    hidden1 = dot(norm1, w_up0)
    active1 = gelu_exact(hidden1).astype(BF)
    second = first + dot_t(active1, w_down0)
    norm2 = layer_norm(second, gain[2]).astype(BF)
    query = heads_of((dot(norm2, w_q) * HEAD ** (-0.5)).astype(BF))
    keys = heads_of(dot(norm2, w_k).astype(BF))
    values = heads_of(dot(norm2, w_v).astype(BF))
    s = jnp.einsum("qhe,khe->hqk", query, keys, preferred_element_type=F32)
    probs = jnp.exp(s - jnp.max(s, -1, keepdims=True))
    probs = probs / jnp.sum(probs, -1, keepdims=True)
    mixed = jnp.einsum("hqk,khe->qhe", probs.astype(BF), values, preferred_element_type=F32)
    mixed = mixed.astype(BF).reshape(n_lat, -1)
    third = second + dot_t(mixed, w_out1)
    norm3 = layer_norm(third, gain[3]).astype(BF)
    w_up1, w_down1, w_dk, w_dv, x_query, w_dq, w_do, w_voc = last_weights()
    hidden3 = dot(norm3, w_up1)
    active3 = gelu_exact(hidden3).astype(BF)
    fourth = third + dot_t(active3, w_down1)
    norm4 = layer_norm(fourth, gain[4]).astype(BF)
    grad_logits = links.free(cot_task())

    dec_keys = dot(norm4, w_dk).astype(BF)
    dec_values = dot(norm4, w_dv).astype(BF)
    key_query = (dot_t(dec_keys, w_dq) * dec_scale).astype(BF)
    value_out = dot(dec_values, w_do).astype(BF)
    value_voc = dot(value_out, w_voc).astype(BF)
    s = dot(key_query, x_query)
    p = jnp.exp(s - jnp.max(s, 0, keepdims=True))
    p = p / jnp.sum(p, 0, keepdims=True)
    p_low = p.astype(BF)
    logits_t = dot_tn(value_voc, p_low).astype(BF)
    d_p = dot(value_voc, grad_logits)
    d_s = (p * (d_p - jnp.sum(d_p * p, 0, keepdims=True))).astype(BF)
    d_vv = dot_t(p_low, grad_logits).astype(BF)
    d_kq = (dot_t(d_s, x_query) * dec_scale).astype(BF)
    d_vo = dot_t(d_vv, w_voc).astype(BF)
    d_dk = dot(d_kq, w_dq).astype(BF)
    d_dv = dot_t(d_vo, w_do).astype(BF)

    def logits_task():
        part = lambda t: lax.dynamic_slice_in_dim(logits_t, links.z_of(t) * rows, rows, 1)
        own = part(0)
        got = yield [("z", mn - t, part(t)) for t in range(1, items)]
        out = jnp.concatenate(([own] + list(got)) * 2, 1)
        first = ((items - mine) % items) * rows
        out = lax.dynamic_slice_in_dim(out, first, items * rows, 1)
        return out.reshape(-1, items, rows).transpose(1, 2, 0)

    def by_columns(value, t):
        size = value.shape[-1] // mn
        return lax.slice_in_dim(value, t * size, (t + 1) * size, axis=value.ndim - 1)

    def by_own_columns(value, t):
        size = value.shape[-1] // mn
        return lax.dynamic_slice_in_dim(value, links.z_of(t) * size, size, value.ndim - 1)

    def by_own_rows(value, t):
        size = value.shape[-2] // mn
        return lax.dynamic_slice_in_dim(value, links.z_of(t) * size, size, value.ndim - 2)

    def summed(*terms):
        whole = jnp.concatenate([term.astype(BF) for term in terms], 1)
        ready = nothing_of(whole)
        whole = lax.psum_scatter(whole, "dp", scatter_dimension=0, tiled=True)
        edge, out = 0, []
        for term in terms:
            out.append(whole[:, edge : edge + term.shape[1]])
            edge += term.shape[1]
        return ready, out

    def columns(terms):
        return links.free(
            links.sum_ring(lambda t: jnp.concatenate([by_own_columns(v, t) for v in terms], 1))
        )

    d_res, d_gain4 = norm_back(fourth, gain[4], dot_t(d_dk, w_dk) + dot_t(d_dv, w_dv))
    d_gain4 = jnp.sum(d_gain4, 0)
    ready, rows_a = summed(
        dot_tn(key_query, d_s),
        dot_tn(d_kq, dec_keys),
        dot_tn(dec_values, d_vo),
        dot_tn(value_out, d_vv),
    )
    d_res = d_res + ready
    g_deck = [dot_tn(norm4, d_dk), dot_tn(norm4, d_dv)]

    def ffn_back(d_res, resid, gain, w_up, w_down, normed, hidden, active):
        branch = d_res.astype(BF)
        d_hidden = (dot(branch, w_down) * gelu_slope(hidden)).astype(BF)
        grads = [dot_tn(normed, d_hidden), dot_tn(branch, active)]
        extra, d_gain = norm_back(resid, gain, dot_t(d_hidden, w_up))
        return d_res + extra, jnp.sum(d_gain, 0), grads

    d_res, d_gain3, g_ffn1 = ffn_back(
        d_res, third, gain[3], w_up1, w_down1, norm3, hidden3, active3
    )

    branch = d_res.astype(BF)
    d_mixed = heads_of(dot(branch, w_out1).astype(BF))
    d_probs = jnp.einsum("qhe,khe->hqk", d_mixed, values, preferred_element_type=F32)
    d_s = (probs * (d_probs - jnp.sum(d_probs * probs, -1, keepdims=True))).astype(BF)
    d_values = jnp.einsum("hqk,qhe->khe", probs.astype(BF), d_mixed, preferred_element_type=F32)
    d_keys = jnp.einsum("hqk,qhe->khe", d_s, query, preferred_element_type=F32)
    d_query = jnp.einsum("hqk,khe->qhe", d_s, keys, preferred_element_type=F32)
    d_values = d_values.astype(BF).reshape(n_lat, -1)
    d_keys = d_keys.astype(BF).reshape(n_lat, -1)
    d_query = (d_query * HEAD ** (-0.5)).astype(BF).reshape(n_lat, -1)
    ready, rows_b = summed(
        *g_deck,
        *g_ffn1,
        dot_tn(norm2, d_values),
        dot_tn(branch, mixed),
        dot_tn(norm2, d_query),
        dot_tn(norm2, d_keys),
    )
    extra, d_gain2 = norm_back(
        second, gain[2], dot_t(d_query, w_q) + dot_t(d_keys, w_k) + dot_t(d_values, w_v)
    )
    d_res, d_gain2 = d_res + extra + ready, jnp.sum(d_gain2, 0)
    d_res, d_gain1, g_ffn0 = ffn_back(
        d_res, first, gain[1], w_up0, w_down0, norm1, hidden1, active1
    )

    branch = d_res.astype(BF)
    d_attended = dot(branch, w_out0).astype(BF)
    mix_grad = dot_t(d_attended, w_value)
    value_term = dot_tn(mix, d_attended).astype(BF).reshape(dn, in_rows, chan)
    value_term = jnp.pad(value_term, ((0, 0), (0, col_rows - in_rows), (0, 0)))
    value_term = value_term.reshape(dn * col_rows, chan)
    ready, rows_c = summed(*g_ffn0, dot_tn(branch, attended), value_term)
    around = links.free(links.ring((mix_grad * repeat + ready).astype(BF)))

    def latents_task():
        value = yield from links.sum_ring(lambda t: by_own_rows(branch, t))
        for bit in chips[::-1] + [1]:
            half = value.shape[1] // 2
            low, high = value[:, :half], value[:, half:]
            up = (d & bit) != 0
            (got,) = yield [(bit, 0, jnp.where(up, low, high).astype(BF))]
            value = jnp.where(up, high, low) + got.astype(F32)
        return value

    g_lat = links.free(latents_task())

    e_all = links.natural_rows(around).reshape(mn, n_lat, -1)[:items]
    norm_probs = weights * share[:, :, None]
    d_probs = jnp.einsum("ild,ird->ilr", e_all, byte_norm, preferred_element_type=F32)
    delta = jnp.sum(norm_probs * d_probs, -1)
    delta = links.free(links.sum_mp(delta))
    d_scores = (norm_probs * (d_probs - delta[:, :, None])).astype(BF)
    d_qk = jnp.einsum("ilr,ird->ld", d_scores, byte_norm, preferred_element_type=F32)
    d_qk = links.free(links.sum_all_rows(d_qk))
    d_bn = jnp.einsum("ilr,ld->ird", d_scores, query_key, preferred_element_type=F32)
    d_bn = d_bn + jnp.einsum(
        "ilr,ild->ird", norm_probs.astype(BF), e_all, preferred_element_type=F32
    )
    d_start, d_byte_gain = norm_back(start, byte_gain_all, d_bn)
    d_bytes = d_start * (1.0 - masked)
    d_mask = jnp.sum(d_start * masked, (0, 1))
    d_byte_gain = jnp.sum(d_byte_gain, (0, 1))
    logits = links.free(logits_task())

    d_query_m = (dot(d_qk, key_w) * enc_scale).astype(BF)
    d_lat_norm = links.free(
        links.sum_ring(
            lambda t, value=dot_t(d_query_m, col_zero).astype(BF): by_own_rows(value, t)
        )
    )
    d_qk_own = lax.dynamic_index_in_dim(d_qk.reshape(n_lat, dn, in_rows), d, 1, False)
    g_key = dot_tn(d_qk_own, query_m)
    lat_mine = lax.dynamic_slice_in_dim(lat_norm, d * col_rows, col_rows, 1)
    g_col0 = dot_tn(lat_mine, d_query_m)
    lat_own = lax.dynamic_slice_in_dim(lat, z * own_lat, own_lat, 0)
    d_lat, d_gain0 = norm_back(lat_own, gain[0], d_lat_norm)

    d_gains = jnp.stack([jnp.sum(d_gain0, 0) / dn, d_gain1, d_gain2, d_gain3, d_gain4])
    sums = jnp.concatenate([d_gains.reshape(-1), d_mask, d_byte_gain]).reshape(-1, 128)
    sums = links.free(links.sum_all(sums)).reshape(-1)
    place = d * mn + z
    g_gains = lax.dynamic_slice_in_dim(
        sums[: n_gain * chan].reshape(n_gain, chan), place * own_gain, own_gain, 1
    )
    g_mask = lax.dynamic_slice_in_dim(sums, n_gain * chan + place * own_in, own_in, 0)
    g_byte_gain = lax.dynamic_slice_in_dim(
        sums, n_gain * chan + wide_in + place * own_in, own_in, 0
    )
    g_lat = g_lat + lax.dynamic_slice_in_dim(d_lat, d * lat_cols, lat_cols, 1)
    split = lambda value, *wides: jnp.split(value, [sum(wides[: i + 1]) for i in range(len(wides) - 1)], 1)

    def rows_task(terms):
        value = jnp.concatenate(terms, 1)
        return links.sum_ring(lambda t: by_own_rows(value, t))

    g_xq, g_dq, g_do, g_voc = rows_a
    g_xq = columns([g_xq])
    g_sq = links.free(rows_task([g_dq, g_do, g_voc]))
    after = nothing_of(g_sq).astype(BF)
    g_b = columns([term + after for term in rows_b])
    g_dk, g_dv, g_up1, g_down1, g_v, g_out1, g_q, g_k = split(
        g_b, *([deck_wide] * 2 + [col_wide] * 6)
    )
    after = nothing_of(g_b).astype(BF)
    g_up0, g_down0, g_out0, g_value = split(columns([term + after for term in rows_c]), *[col_wide] * 4)
    g_value = g_value[:in_rows]
    return (
        logits,
        d_bytes,
        g_lat,
        jnp.stack([g_col0, g_up0, g_q, g_k, g_v, g_up1]),
        jnp.stack([g_out0, g_out1]),
        jnp.stack([g_down0, g_down1]),
        jnp.stack([g_key, g_value]),
        jnp.stack([g_dk, g_dv]),
        g_xq.T,
        jnp.stack([g_sq[:, :wide_in], g_sq[:, wide_in : 2 * wide_in]]),
        g_sq[:, 2 * wide_in :],
        g_gains,
        g_mask,
        g_byte_gain,
    )


def solution(mesh):
    return jax.shard_map(
        functools.partial(per_device, mesh.shape["dp"], mesh.shape["mp"]),
        mesh=mesh,
        in_specs=(
            P("dp", "mp", None),
            P("dp"),
            P("dp", None),
            P("dp", None),
            P("mp", "dp"),
            P(None, "dp", "mp"),
            P(None, "dp", "mp"),
            P(None, "dp", "mp"),
            P(None, "dp", "mp"),
            P(None, "dp", "mp"),
            P("mp", "dp"),
            P(None, ("dp", "mp"), None),
            P(("dp", "mp"), None),
            P(None, ("dp", "mp")),
            P(("dp", "mp")),
            P(("dp", "mp")),
            P("dp", "mp", None),
        ),
        out_specs=(
            P("dp", "mp", None),
            P("dp", "mp", None),
            P("mp", "dp"),
            P(None, "dp", "mp"),
            P(None, "dp", "mp"),
            P(None, "dp", "mp"),
            P(None, "dp", "mp"),
            P(None, "dp", "mp"),
            P("mp", "dp"),
            P(None, ("dp", "mp"), None),
            P(("dp", "mp"), None),
            P(None, ("dp", "mp")),
            P(("dp", "mp")),
            P(("dp", "mp")),
        ),
        check_vma=False,
    )
```

```python
import functools
import math

import jax
import jax.numpy as jnp
from jax import lax
from jax.sharding import PartitionSpec as P

HEAD = 160
BF = jnp.bfloat16
F32 = jnp.float32


def dot(left, right):
    return jnp.dot(left, right, preferred_element_type=F32)


def dot_t(left, right):
    return lax.dot_general(
        left,
        right,
        (((left.ndim - 1,), (right.ndim - 1,)), ((), ())),
        preferred_element_type=F32,
    )


def dot_tn(left, right):
    return lax.dot_general(left, right, (((0,), (0,)), ((), ())), preferred_element_type=F32)


def layer_norm(value, gain):
    centre = value - jnp.mean(value, -1, keepdims=True)
    spread_sq = jnp.mean(centre * centre, -1, keepdims=True)
    return centre * lax.rsqrt(spread_sq + 1e-05) * gain


def norm_back(value, gain, grad):
    centre = value - jnp.mean(value, -1, keepdims=True)
    inv = lax.rsqrt(jnp.mean(centre * centre, -1, keepdims=True) + 1e-05)
    unit = centre * inv
    scaled = grad * gain
    d_value = inv * (
        scaled
        - jnp.mean(scaled, -1, keepdims=True)
        - unit * jnp.mean(scaled * unit, -1, keepdims=True)
    )
    return d_value, grad * unit


def masked_rows(ratio, starts, lengths, positions):
    spaced = positions * 73 % 100 < ratio
    within = (positions[:, None] >= starts[None, :]) & (
        positions[:, None] < starts[None, :] + lengths[None, :]
    )
    return jnp.where(spaced | jnp.any(within, axis=1), 1.0, 0.0).astype(F32)


def gelu_exact(value):
    return jax.nn.gelu(value, approximate=False)


def gelu_slope(value):
    return 0.5 * (1.0 + lax.erf(value * 0.7071067811865476)) + value * 0.3989422804014327 * jnp.exp(
        -0.5 * value * value
    )


def nothing_of(value):
    return value[0, 0].astype(F32) * 0.0


class Links:
    def __init__(self, dn, mn):
        self.dn, self.mn = dn, mn
        self.bits = dn.bit_length() - 1
        assert 1 << self.bits == dn and mn & (mn - 1) == 0
        self.chips = [1 << b for b in range(1, self.bits)]
        self.d = lax.axis_index("dp")
        self.z = lax.axis_index("mp")

    def z_of(self, t):
        return (self.z - t) % self.mn

    def ring(self, value):
        parts = [value]
        for _ in range(self.mn - 1):
            parts += yield [("z", 1, parts[-1])]
        return parts

    def direct(self, values):
        got = yield [("z", t, values[t]) for t in range(1, self.mn)]
        return [values[0]] + list(got)

    def natural_z(self, parts):
        shape = parts[0].shape
        size = math.prod(shape[:-1])
        around = [parts[(-k) % self.mn].reshape(size, shape[-1]) for k in range(self.mn)] * 2
        first = ((self.mn - self.z) % self.mn) * size
        whole = lax.dynamic_slice_in_dim(jnp.concatenate(around, 0), first, self.mn * size, 0)
        return [whole[k * size : (k + 1) * size].reshape(shape) for k in range(self.mn)]

    def natural_rows(self, parts):
        size = parts[0].shape[0]
        around = jnp.concatenate([parts[(-k) % self.mn] for k in range(self.mn)] * 2, 0)
        return lax.dynamic_slice_in_dim(
            around, ((self.mn - self.z) % self.mn) * size, self.mn * size, 0
        )

    def natural_columns(self, parts):
        size = parts[0].shape[1]
        around = jnp.concatenate([parts[(-k) % self.mn] for k in range(self.mn)] * 2, 1)
        return lax.dynamic_slice_in_dim(
            around, ((self.mn - self.z) % self.mn) * size, self.mn * size, 1
        )

    def free(self, steps):
        got = None
        while True:
            try:
                sends = steps.send(got)
            except StopIteration as end:
                return end.value
            got = [self.send(*send) for send in sends]

    def send(self, lane, move, value):
        if lane == "z":
            pairs = [(i, (i + move) % self.mn) for i in range(self.mn)]
            return lax.ppermute(value, "mp", pairs)
        return lax.ppermute(value, "dp", [(i, i ^ lane) for i in range(self.dn)])

    def by_index(self, value):
        value = value.reshape((2,) * self.bits + value.shape[1:])
        for axis in range(self.bits):
            up = (self.d >> (self.bits - 1 - axis)) & 1
            value = jnp.where(up == 1, jnp.flip(value, axis), value)
        return value.reshape((self.dn,) + value.shape[self.bits :])

    def spread(self, piece, turned):
        pieces = {0: piece}
        ready = []
        for bit in turned:
            for key in list(pieces):
                mates, ready = ready, []
                got = yield [(bit, 0, pieces[key])] + [(1, 0, pieces[k]) for k in mates]
                pieces[key ^ bit] = got[0]
                pieces.update({k ^ 1: v for k, v in zip(mates, got[1:])})
                ready = [key ^ bit] + ([0] if key == 0 and bit == turned[0] else [])
        got = yield [(1, 0, pieces[k]) for k in ready]
        pieces.update({k ^ 1: v for k, v in zip(ready, got)})
        return pieces

    def sum_ring(self, block):
        total = block(1).astype(BF)
        for t in range(2, self.mn):
            (got,) = yield [("z", 1, total)]
            total = (got.astype(F32) + block(t).astype(F32)).astype(BF)
        (got,) = yield [("z", 1, total)]
        return got.astype(F32) + block(0).astype(F32)

    def sum_split(self, block):
        got = yield [("z", t, block(self.mn - t).astype(BF)) for t in range(1, self.mn)]
        return block(0).astype(F32) + sum(part.astype(F32) for part in got)

    def sum_mp(self, value):
        got = yield from self.direct([value] * self.mn)
        return sum(self.natural_z(got))

    def sum_mp_rows(self, value):
        size = value.shape[0] // self.mn
        parts = [
            lax.dynamic_slice_in_dim(value, ((self.z + t) % self.mn) * size, size, 0).astype(BF)
            for t in range(self.mn)
        ]
        got = yield from self.direct(parts)
        total = sum(part.astype(F32) for part in got).astype(BF)
        got = yield from self.direct([total] * self.mn)
        return self.natural_rows(got)

    def sum_all(self, value):
        for bit in [1] + self.chips:
            (got,) = yield [(bit, 0, value)]
            value = value + got
        return (yield from self.sum_mp(value))

    def sum_all_rows(self, value):
        for b in range(self.bits):
            half = value.shape[0] // 2
            low, high = value[:half], value[half:]
            up = (self.d >> b) & 1
            give = jnp.where(up == 1, low, high).astype(BF)
            (got,) = yield [(1 << b, 0, give)]
            value = jnp.where(up == 1, high, low) + got.astype(F32)
        value = value.astype(BF)
        value = yield from self.direct([value] * self.mn)
        size = value[0].shape[0]
        value = self.natural_rows(value).astype(F32)
        value = sum(value[k * size : (k + 1) * size] for k in range(self.mn)).astype(BF)
        for b in reversed(range(self.bits)):
            (other,) = yield [(1 << b, 0, value)]
            up = (self.d >> b) & 1
            value = jnp.concatenate(
                [jnp.where(up == 1, other, value), jnp.where(up == 1, value, other)], 0
            )
        return value


def heads_of(value):
    return value.reshape(value.shape[0], -1, HEAD)


def per_device(
    dn,
    mn,
    bytes_in,
    mask_ratio,
    mask_starts,
    mask_lengths,
    latents,
    col,
    attn_out,
    mlp_down,
    enc_kv,
    dec_kv,
    dec_queries,
    dec_square,
    vocab,
    gains,
    mask_vec,
    byte_gain,
    cotangent,
):
    links = Links(dn, mn)
    d, z = links.d, links.z
    items, rows, wide_in = bytes_in.shape
    repeat = mn // items
    assert repeat * items == mn
    seq = rows * mn
    mine = z % items
    chan = col.shape[1] * dn
    enc_scale = chan ** (-0.5)
    dec_scale = wide_in ** (-0.5)

    n_gain, own_gain = gains.shape
    own_in = mask_vec.shape[0]
    in_rows = enc_kv.shape[1]
    col_rows, col_wide = col.shape[1:]
    own_lat, lat_cols = latents.shape
    small = jnp.concatenate([gains.reshape(-1), mask_vec, byte_gain])
    n_small = small.shape[0]
    line = jnp.pad(small, (0, -n_small % lat_cols)).reshape(-1, lat_cols)
    line = jnp.pad(line, ((0, -line.shape[0] % max(16 // mn, 1)), (0, 0)))
    chips = links.chips

    def head_task():
        early = yield from links.direct([jnp.concatenate([latents, line], 0)] * mn)
        early = links.natural_z(early)
        lat = [part[:own_lat] for part in early]
        tall = jnp.concatenate([part[own_lat:] for part in early] + lat, 0)
        n_line = tall.shape[0] - own_lat * mn
        heavy = jnp.concatenate([col[0], enc_kv[0]], 0)
        heavy = jnp.pad(heavy, ((n_line, own_lat * mn - heavy.shape[0]), (0, 0)))
        return (yield from links.spread(jnp.concatenate([tall, heavy], 1), chips))

    cat = lambda parts: jnp.concatenate(parts, -1)

    own_sq = dec_square.shape[1]
    n_voc = vocab.shape[1]
    deck_wide = dec_kv.shape[2]
    own_query, own_pos = dec_queries.T.shape

    def gathered(parts, wide):
        parts = [jnp.pad(p, ((0, -p.shape[0] % 16), (0, wide - p.shape[1]))) for p in parts]
        whole = jnp.concatenate(parts, 0)
        tall = whole.shape[0]
        whole = lax.all_gather(whole, ("dp", "mp"), axis=0, tiled=True)
        whole = whole.reshape(dn, mn, tall, wide)
        edges = [0]
        for p in parts:
            edges.append(edges[-1] + p.shape[0])
        return whole, edges

    def beside(got, row, col, size, wide):
        parts = [got[:, m, row : row + size, col : col + wide] for m in range(mn)]
        return jnp.concatenate([part.reshape(dn * size, wide) for part in parts], 1)

    side = lambda *parts: jnp.concatenate(parts, 1)
    w_one, at_one = gathered(
        [
            side(attn_out[0], col[1]),
            side(mlp_down[0], col[2]),
            side(col[3], col[4]),
            side(attn_out[1], jnp.pad(enc_kv[1], ((0, col_rows - in_rows), (0, 0)))),
        ],
        2 * col_wide,
    )
    late_wide = 2 * (col_wide + deck_wide)
    sq = side(dec_square[0], dec_square[1], vocab)
    sq = jnp.pad(sq, ((0, -own_sq % 16), (0, -sq.shape[1] % late_wide)))
    halves = 2 if own_query % 32 == 0 and 2 * own_pos <= late_wide else 1
    part_rows = own_query // halves
    def first_weight(k):
        return beside(w_one, at_one[k // 2], (k % 2) * col_wide, col_rows, col_wide)

    def last_weights():
        edge = 0
        out = []
        for wide in (col_wide, col_wide, deck_wide, deck_wide):
            out.append(beside(w_two, 0, edge, col_rows, wide))
            edge += wide
        query = [
            w_two[:, :, at_two[1] : at_two[1] + part_rows, h * own_pos : (h + 1) * own_pos]
            for h in range(halves)
        ]
        query = jnp.stack(query, 1).transpose(0, 1, 3, 2, 4).reshape(dn * own_query, seq)
        lines = jnp.concatenate(
            [w_two[:, :, row : row + own_sq] for row in at_two[2:-1]], -1
        ).reshape(dn * mn * own_sq, -1)
        return out + [
            query,
            lines[:, :wide_in],
            lines[:, wide_in : 2 * wide_in],
            lines[:, 2 * wide_in : 2 * wide_in + n_voc],
        ]

    steps = jnp.arange(rows, dtype=jnp.int32)
    masked = jax.vmap(lambda a, b, c: masked_rows(a, b, c, z * rows + steps))(
        mask_ratio, mask_starts, mask_lengths
    )[:, :, None]
    masked_item = masked_rows(
        mask_ratio[mine], mask_starts[mine], mask_lengths[mine], jnp.arange(seq, dtype=jnp.int32)
    )
    cot = cotangent.swapaxes(1, 2)
    head = links.free(head_task())
    held = links.by_index(jnp.stack([head[r] for r in range(dn)]))

    late_parts = [
        side(col[5], mlp_down[1], dec_kv[0], dec_kv[1]),
        jnp.concatenate(jnp.split(dec_queries.T, halves, 0), 1),
    ] + jnp.split(sq, sq.shape[1] // late_wide, 1)
    n_lat = own_lat * mn
    n_line = line.shape[0] * mn
    smalls = held[:, :n_line, :lat_cols].reshape(dn, mn, -1)[:, :, :n_small].astype(F32)
    gain = smalls[:, :, : n_gain * own_gain].reshape(dn, mn, n_gain, own_gain)
    gain = gain.transpose(2, 0, 1, 3).reshape(n_gain, -1)
    vecs = smalls[:, :, n_gain * own_gain :]
    mask_all = vecs[:, :, :own_in].reshape(-1)
    byte_gain_all = vecs[:, :, own_in:].reshape(-1)
    lat = held[:, n_line:, :lat_cols].transpose(1, 0, 2).reshape(n_lat, -1).astype(F32)
    col_zero = held[:, n_line : n_line + col_rows, lat_cols:].reshape(dn * col_rows, -1)
    key_w = held[:, n_line + col_rows : n_line + col_rows + in_rows, lat_cols:]
    key_w = key_w.reshape(dn * in_rows, -1)
    lat_norm = layer_norm(lat, gain[0]).astype(BF)
    query_m = (dot(lat_norm, col_zero) * enc_scale).astype(BF)
    query_key = dot_t(query_m, key_w)
    query_key = links.free(links.sum_mp_rows(query_key))

    raw = bytes_in.astype(F32)
    start = raw + masked * (mask_all - raw)
    byte_norm = layer_norm(start, byte_gain_all).astype(BF)

    scores = jnp.einsum("ld,ird->ilr", query_key, byte_norm, preferred_element_type=F32)
    top = jnp.max(scores, -1)
    weights = jnp.exp(scores - top[:, :, None])
    below = jnp.sum(weights, -1)
    mix = jnp.einsum("ilr,ird->ild", weights.astype(BF), byte_norm, preferred_element_type=F32)
    mix = mix.astype(BF)

    def mix_task(mix, top, below):
        block = lambda t: lax.dynamic_index_in_dim(mix, links.z_of(t) % items, 0, False)
        pack = jnp.stack([top, below])
        got = yield [("z", t, pack) for t in range(1, mn)] + [("z", 1, block(1))]
        stats = jnp.stack([pack] + list(got[: mn - 1]))
        top_all = jnp.max(stats[:, 0], 0)
        shares = jnp.exp(stats[:, 0] - top_all)
        total = sum(links.natural_z(list(stats[:, 1] * shares)))
        pick = lambda t, i: lax.dynamic_index_in_dim(shares[t], i % items, 0, False)[:, None]
        arrived = got[-1].astype(F32) * pick(1 % mn, links.z_of(2))
        for t in range(2, mn):
            arrived = (arrived + block(t).astype(F32) * pick(0, links.z_of(t))).astype(BF)
            (arrived,) = yield [("z", 1, arrived)]
            arrived = arrived.astype(F32)
        whole = arrived + block(0).astype(F32) * pick(0, z)
        whole = whole / lax.dynamic_index_in_dim(total, mine, 0, False)[:, None]
        return whole.astype(BF), shares[0] / total

    assert mn > 2
    mix, share = links.free(mix_task(mix, top, below))
    w_out0, w_up0, w_down0, w_q, w_k, w_v, w_out1 = (first_weight(k) for k in range(7))
    w_value = beside(w_one, at_one[3], col_wide, in_rows, col_wide)
    late_parts[0] = late_parts[0] + (nothing_of(w_one[0, 0]) + nothing_of(mix)).astype(BF)
    w_two, at_two = gathered(
        late_parts,
        late_wide,
    )


    def cot_task():
        held = cot + nothing_of(w_two[0, 0]).astype(BF)
        parts = [lax.dynamic_index_in_dim(held, (z + t) % mn % items, 0, False) for t in range(mn)]
        parts = yield from links.direct(parts)
        return (links.natural_columns(parts).astype(F32) * (masked_item / repeat)[None, :]).astype(BF)

    attended = dot(mix, w_value).astype(BF)
    first = lat + dot_t(attended, w_out0)
    norm1 = layer_norm(first, gain[1]).astype(BF)
    hidden1 = dot(norm1, w_up0)
    active1 = gelu_exact(hidden1).astype(BF)
    second = first + dot_t(active1, w_down0)
    norm2 = layer_norm(second, gain[2]).astype(BF)
    query = heads_of((dot(norm2, w_q) * HEAD ** (-0.5)).astype(BF))
    keys = heads_of(dot(norm2, w_k).astype(BF))
    values = heads_of(dot(norm2, w_v).astype(BF))
    s = jnp.einsum("qhe,khe->hqk", query, keys, preferred_element_type=F32)
    probs = jnp.exp(s - jnp.max(s, -1, keepdims=True))
    probs = probs / jnp.sum(probs, -1, keepdims=True)
    mixed = jnp.einsum("hqk,khe->qhe", probs.astype(BF), values, preferred_element_type=F32)
    mixed = mixed.astype(BF).reshape(n_lat, -1)
    third = second + dot_t(mixed, w_out1)
    norm3 = layer_norm(third, gain[3]).astype(BF)
    w_up1, w_down1, w_dk, w_dv, x_query, w_dq, w_do, w_voc = last_weights()
    hidden3 = dot(norm3, w_up1)
    active3 = gelu_exact(hidden3).astype(BF)
    fourth = third + dot_t(active3, w_down1)
    norm4 = layer_norm(fourth, gain[4]).astype(BF)
    grad_logits = links.free(cot_task())

    dec_keys = dot(norm4, w_dk).astype(BF)
    dec_values = dot(norm4, w_dv).astype(BF)
    key_query = (dot_t(dec_keys, w_dq) * dec_scale).astype(BF)
    value_out = dot(dec_values, w_do).astype(BF)
    value_voc = dot(value_out, w_voc).astype(BF)
    s = dot(key_query, x_query)
    p = jnp.exp(s - jnp.max(s, 0, keepdims=True))
    p = p / jnp.sum(p, 0, keepdims=True)
    p_low = p.astype(BF)
    logits_t = dot_tn(value_voc, p_low).astype(BF)
    d_p = dot(value_voc, grad_logits)
    d_s = (p * (d_p - jnp.sum(d_p * p, 0, keepdims=True))).astype(BF)
    d_vv = dot_t(p_low, grad_logits).astype(BF)
    d_kq = (dot_t(d_s, x_query) * dec_scale).astype(BF)
    d_vo = dot_t(d_vv, w_voc).astype(BF)
    d_dk = dot(d_kq, w_dq).astype(BF)
    d_dv = dot_t(d_vo, w_do).astype(BF)

    def logits_task():
        part = lambda t: lax.dynamic_slice_in_dim(logits_t, links.z_of(t) * rows, rows, 1)
        own = part(0)
        got = yield [("z", mn - t, part(t)) for t in range(1, items)]
        out = jnp.concatenate(([own] + list(got)) * 2, 1)
        first = ((items - mine) % items) * rows
        out = lax.dynamic_slice_in_dim(out, first, items * rows, 1)
        return out.reshape(-1, items, rows).transpose(1, 2, 0)

    def by_columns(value, t):
        size = value.shape[-1] // mn
        return lax.slice_in_dim(value, t * size, (t + 1) * size, axis=value.ndim - 1)

    def by_own_columns(value, t):
        size = value.shape[-1] // mn
        return lax.dynamic_slice_in_dim(value, links.z_of(t) * size, size, value.ndim - 1)

    def by_own_rows(value, t):
        size = value.shape[-2] // mn
        return lax.dynamic_slice_in_dim(value, links.z_of(t) * size, size, value.ndim - 2)

    def summed(*terms):
        whole = jnp.concatenate([term.astype(BF) for term in terms], 1)
        ready = nothing_of(whole)
        whole = lax.psum_scatter(whole, "dp", scatter_dimension=0, tiled=True)
        edge, out = 0, []
        for term in terms:
            out.append(whole[:, edge : edge + term.shape[1]])
            edge += term.shape[1]
        return ready, out

    def last_columns(terms):
        return links.free(
            links.sum_split(lambda t: jnp.concatenate([by_own_columns(v, t) for v in terms], 1))
        )

    def columns(terms):
        return links.free(
            links.sum_ring(lambda t: jnp.concatenate([by_own_columns(v, t) for v in terms], 1))
        )

    d_res, d_gain4 = norm_back(fourth, gain[4], dot_t(d_dk, w_dk) + dot_t(d_dv, w_dv))
    d_gain4 = jnp.sum(d_gain4, 0)
    ready, rows_a = summed(
        dot_tn(key_query, d_s),
        dot_tn(d_kq, dec_keys),
        dot_tn(dec_values, d_vo),
        dot_tn(value_out, d_vv),
    )
    d_res = d_res + ready
    g_deck = [dot_tn(norm4, d_dk), dot_tn(norm4, d_dv)]

    def ffn_back(d_res, resid, gain, w_up, w_down, normed, hidden, active):
        branch = d_res.astype(BF)
        d_hidden = (dot(branch, w_down) * gelu_slope(hidden)).astype(BF)
        grads = [dot_tn(normed, d_hidden), dot_tn(branch, active)]
        extra, d_gain = norm_back(resid, gain, dot_t(d_hidden, w_up))
        return d_res + extra, jnp.sum(d_gain, 0), grads

    d_res, d_gain3, g_ffn1 = ffn_back(
        d_res, third, gain[3], w_up1, w_down1, norm3, hidden3, active3
    )

    branch = d_res.astype(BF)
    d_mixed = heads_of(dot(branch, w_out1).astype(BF))
    d_probs = jnp.einsum("qhe,khe->hqk", d_mixed, values, preferred_element_type=F32)
    d_s = (probs * (d_probs - jnp.sum(d_probs * probs, -1, keepdims=True))).astype(BF)
    d_values = jnp.einsum("hqk,qhe->khe", probs.astype(BF), d_mixed, preferred_element_type=F32)
    d_keys = jnp.einsum("hqk,qhe->khe", d_s, query, preferred_element_type=F32)
    d_query = jnp.einsum("hqk,khe->qhe", d_s, keys, preferred_element_type=F32)
    d_values = d_values.astype(BF).reshape(n_lat, -1)
    d_keys = d_keys.astype(BF).reshape(n_lat, -1)
    d_query = (d_query * HEAD ** (-0.5)).astype(BF).reshape(n_lat, -1)
    ready, rows_b = summed(
        *g_deck,
        *g_ffn1,
        dot_tn(norm2, d_values),
        dot_tn(branch, mixed),
        dot_tn(norm2, d_query),
        dot_tn(norm2, d_keys),
    )
    extra, d_gain2 = norm_back(
        second, gain[2], dot_t(d_query, w_q) + dot_t(d_keys, w_k) + dot_t(d_values, w_v)
    )
    d_res, d_gain2 = d_res + extra + ready, jnp.sum(d_gain2, 0)
    d_res, d_gain1, g_ffn0 = ffn_back(
        d_res, first, gain[1], w_up0, w_down0, norm1, hidden1, active1
    )

    branch = d_res.astype(BF)
    d_attended = dot(branch, w_out0).astype(BF)
    mix_grad = dot_t(d_attended, w_value)
    value_term = dot_tn(mix, d_attended).astype(BF).reshape(dn, in_rows, chan)
    value_term = jnp.pad(value_term, ((0, 0), (0, col_rows - in_rows), (0, 0)))
    value_term = value_term.reshape(dn * col_rows, chan)
    ready, rows_c = summed(*g_ffn0, dot_tn(branch, attended), value_term)
    around = links.free(links.ring((mix_grad * repeat + ready).astype(BF)))

    def latents_task():
        value = yield from links.sum_ring(lambda t: by_own_rows(branch, t))
        for bit in chips[::-1] + [1]:
            half = value.shape[1] // 2
            low, high = value[:, :half], value[:, half:]
            up = (d & bit) != 0
            (got,) = yield [(bit, 0, jnp.where(up, low, high).astype(BF))]
            value = jnp.where(up, high, low) + got.astype(F32)
        return value

    g_lat = links.free(latents_task())

    e_all = links.natural_rows(around).reshape(mn, n_lat, -1)[:items]
    norm_probs = weights * share[:, :, None]
    d_probs = jnp.einsum("ild,ird->ilr", e_all, byte_norm, preferred_element_type=F32)
    delta = jnp.sum(norm_probs * d_probs, -1)
    delta = links.free(links.sum_mp(delta))
    d_scores = (norm_probs * (d_probs - delta[:, :, None])).astype(BF)
    d_qk = jnp.einsum("ilr,ird->ld", d_scores, byte_norm, preferred_element_type=F32)
    d_qk = links.free(links.sum_all_rows(d_qk))
    d_bn = jnp.einsum("ilr,ld->ird", d_scores, query_key, preferred_element_type=F32)
    d_bn = d_bn + jnp.einsum(
        "ilr,ild->ird", norm_probs.astype(BF), e_all, preferred_element_type=F32
    )
    d_start, d_byte_gain = norm_back(start, byte_gain_all, d_bn)
    d_bytes = d_start * (1.0 - masked)
    d_mask = jnp.sum(d_start * masked, (0, 1))
    d_byte_gain = jnp.sum(d_byte_gain, (0, 1))
    logits = links.free(logits_task())

    d_query_m = (dot(d_qk, key_w) * enc_scale).astype(BF)
    d_lat_norm = links.free(
        links.sum_ring(
            lambda t, value=dot_t(d_query_m, col_zero).astype(BF): by_own_rows(value, t)
        )
    )
    d_qk_own = lax.dynamic_index_in_dim(d_qk.reshape(n_lat, dn, in_rows), d, 1, False)
    g_key = dot_tn(d_qk_own, query_m)
    lat_mine = lax.dynamic_slice_in_dim(lat_norm, d * col_rows, col_rows, 1)
    g_col0 = dot_tn(lat_mine, d_query_m)
    lat_own = lax.dynamic_slice_in_dim(lat, z * own_lat, own_lat, 0)
    d_lat, d_gain0 = norm_back(lat_own, gain[0], d_lat_norm)

    d_gains = jnp.stack([jnp.sum(d_gain0, 0) / dn, d_gain1, d_gain2, d_gain3, d_gain4])
    sums = jnp.concatenate([d_gains.reshape(-1), d_mask, d_byte_gain]).reshape(-1, 128)
    sums = links.free(links.sum_all(sums)).reshape(-1)
    place = d * mn + z
    g_gains = lax.dynamic_slice_in_dim(
        sums[: n_gain * chan].reshape(n_gain, chan), place * own_gain, own_gain, 1
    )
    g_mask = lax.dynamic_slice_in_dim(sums, n_gain * chan + place * own_in, own_in, 0)
    g_byte_gain = lax.dynamic_slice_in_dim(
        sums, n_gain * chan + wide_in + place * own_in, own_in, 0
    )
    g_lat = g_lat + lax.dynamic_slice_in_dim(d_lat, d * lat_cols, lat_cols, 1)
    split = lambda value, *wides: jnp.split(value, [sum(wides[: i + 1]) for i in range(len(wides) - 1)], 1)

    def rows_task(terms):
        value = jnp.concatenate(terms, 1)
        return links.sum_ring(lambda t: by_own_rows(value, t))

    g_xq, g_dq, g_do, g_voc = rows_a
    g_xq = columns([g_xq])
    g_sq = links.free(rows_task([g_dq, g_do, g_voc]))
    after = nothing_of(g_sq).astype(BF)
    g_b = columns([term + after for term in rows_b])
    g_dk, g_dv, g_up1, g_down1, g_v, g_out1, g_q, g_k = split(
        g_b, *([deck_wide] * 2 + [col_wide] * 6)
    )
    after = nothing_of(g_b).astype(BF)
    g_up0, g_down0, g_out0, g_value = split(last_columns([term + after for term in rows_c]), *[col_wide] * 4)
    g_value = g_value[:in_rows]
    return (
        logits,
        d_bytes,
        g_lat,
        jnp.stack([g_col0, g_up0, g_q, g_k, g_v, g_up1]),
        jnp.stack([g_out0, g_out1]),
        jnp.stack([g_down0, g_down1]),
        jnp.stack([g_key, g_value]),
        jnp.stack([g_dk, g_dv]),
        g_xq.T,
        jnp.stack([g_sq[:, :wide_in], g_sq[:, wide_in : 2 * wide_in]]),
        g_sq[:, 2 * wide_in :],
        g_gains,
        g_mask,
        g_byte_gain,
    )


def solution(mesh):
    return jax.shard_map(
        functools.partial(per_device, mesh.shape["dp"], mesh.shape["mp"]),
        mesh=mesh,
        in_specs=(
            P("dp", "mp", None),
            P("dp"),
            P("dp", None),
            P("dp", None),
            P("mp", "dp"),
            P(None, "dp", "mp"),
            P(None, "dp", "mp"),
            P(None, "dp", "mp"),
            P(None, "dp", "mp"),
            P(None, "dp", "mp"),
            P("mp", "dp"),
            P(None, ("dp", "mp"), None),
            P(("dp", "mp"), None),
            P(None, ("dp", "mp")),
            P(("dp", "mp")),
            P(("dp", "mp")),
            P("dp", "mp", None),
        ),
        out_specs=(
            P("dp", "mp", None),
            P("dp", "mp", None),
            P("mp", "dp"),
            P(None, "dp", "mp"),
            P(None, "dp", "mp"),
            P(None, "dp", "mp"),
            P(None, "dp", "mp"),
            P(None, "dp", "mp"),
            P("mp", "dp"),
            P(None, ("dp", "mp"), None),
            P(("dp", "mp"), None),
            P(None, ("dp", "mp")),
            P(("dp", "mp")),
            P(("dp", "mp")),
        ),
        check_vma=False,
    )
```

```python
import functools
import math

import jax
import jax.numpy as jnp
from jax import lax
from jax.sharding import PartitionSpec as P

HEAD = 160
BF = jnp.bfloat16
F32 = jnp.float32


def dot(left, right):
    return jnp.dot(left, right, preferred_element_type=F32)


def dot_t(left, right):
    return lax.dot_general(
        left,
        right,
        (((left.ndim - 1,), (right.ndim - 1,)), ((), ())),
        preferred_element_type=F32,
    )


def dot_tn(left, right):
    return lax.dot_general(left, right, (((0,), (0,)), ((), ())), preferred_element_type=F32)


def layer_norm(value, gain):
    centre = value - jnp.mean(value, -1, keepdims=True)
    spread_sq = jnp.mean(centre * centre, -1, keepdims=True)
    return centre * lax.rsqrt(spread_sq + 1e-05) * gain


def norm_back(value, gain, grad):
    centre = value - jnp.mean(value, -1, keepdims=True)
    inv = lax.rsqrt(jnp.mean(centre * centre, -1, keepdims=True) + 1e-05)
    unit = centre * inv
    scaled = grad * gain
    d_value = inv * (
        scaled
        - jnp.mean(scaled, -1, keepdims=True)
        - unit * jnp.mean(scaled * unit, -1, keepdims=True)
    )
    return d_value, grad * unit


def masked_rows(ratio, starts, lengths, positions):
    spaced = positions * 73 % 100 < ratio
    within = (positions[:, None] >= starts[None, :]) & (
        positions[:, None] < starts[None, :] + lengths[None, :]
    )
    return jnp.where(spaced | jnp.any(within, axis=1), 1.0, 0.0).astype(F32)


def gelu_exact(value):
    return jax.nn.gelu(value, approximate=False)


def gelu_slope(value):
    return 0.5 * (1.0 + lax.erf(value * 0.7071067811865476)) + value * 0.3989422804014327 * jnp.exp(
        -0.5 * value * value
    )


def nothing_of(value):
    return value[0, 0].astype(F32) * 0.0


class Links:
    def __init__(self, dn, mn):
        self.dn, self.mn = dn, mn
        self.bits = dn.bit_length() - 1
        assert 1 << self.bits == dn and mn & (mn - 1) == 0
        self.chips = [1 << b for b in range(1, self.bits)]
        self.d = lax.axis_index("dp")
        self.z = lax.axis_index("mp")

    def z_of(self, t):
        return (self.z - t) % self.mn

    def ring(self, value):
        parts = [value]
        for _ in range(self.mn - 1):
            parts += yield [("z", 1, parts[-1])]
        return parts

    def direct(self, values):
        got = yield [("z", t, values[t]) for t in range(1, self.mn)]
        return [values[0]] + list(got)

    def natural_z(self, parts):
        shape = parts[0].shape
        size = math.prod(shape[:-1])
        around = [parts[(-k) % self.mn].reshape(size, shape[-1]) for k in range(self.mn)] * 2
        first = ((self.mn - self.z) % self.mn) * size
        whole = lax.dynamic_slice_in_dim(jnp.concatenate(around, 0), first, self.mn * size, 0)
        return [whole[k * size : (k + 1) * size].reshape(shape) for k in range(self.mn)]

    def natural_rows(self, parts):
        size = parts[0].shape[0]
        around = jnp.concatenate([parts[(-k) % self.mn] for k in range(self.mn)] * 2, 0)
        return lax.dynamic_slice_in_dim(
            around, ((self.mn - self.z) % self.mn) * size, self.mn * size, 0
        )

    def natural_columns(self, parts):
        size = parts[0].shape[1]
        around = jnp.concatenate([parts[(-k) % self.mn] for k in range(self.mn)] * 2, 1)
        return lax.dynamic_slice_in_dim(
            around, ((self.mn - self.z) % self.mn) * size, self.mn * size, 1
        )

    def free(self, steps):
        got = None
        while True:
            try:
                sends = steps.send(got)
            except StopIteration as end:
                return end.value
            got = [self.send(*send) for send in sends]

    def send(self, lane, move, value):
        if lane == "z":
            pairs = [(i, (i + move) % self.mn) for i in range(self.mn)]
            return lax.ppermute(value, "mp", pairs)
        return lax.ppermute(value, "dp", [(i, i ^ lane) for i in range(self.dn)])

    def by_index(self, value):
        value = value.reshape((2,) * self.bits + value.shape[1:])
        for axis in range(self.bits):
            up = (self.d >> (self.bits - 1 - axis)) & 1
            value = jnp.where(up == 1, jnp.flip(value, axis), value)
        return value.reshape((self.dn,) + value.shape[self.bits :])

    def spread(self, piece, turned):
        pieces = {0: piece}
        ready = []
        for bit in turned:
            for key in list(pieces):
                mates, ready = ready, []
                got = yield [(bit, 0, pieces[key])] + [(1, 0, pieces[k]) for k in mates]
                pieces[key ^ bit] = got[0]
                pieces.update({k ^ 1: v for k, v in zip(mates, got[1:])})
                ready = [key ^ bit] + ([0] if key == 0 and bit == turned[0] else [])
        got = yield [(1, 0, pieces[k]) for k in ready]
        pieces.update({k ^ 1: v for k, v in zip(ready, got)})
        return pieces

    def sum_ring(self, block):
        total = block(1).astype(BF)
        for t in range(2, self.mn):
            (got,) = yield [("z", 1, total)]
            total = (got.astype(F32) + block(t).astype(F32)).astype(BF)
        (got,) = yield [("z", 1, total)]
        return got.astype(F32) + block(0).astype(F32)

    def sum_split(self, block):
        got = yield [("z", t, block(self.mn - t).astype(BF)) for t in range(1, self.mn)]
        return block(0).astype(F32) + sum(part.astype(F32) for part in got)

    def sum_mp(self, value):
        got = yield from self.direct([value] * self.mn)
        return sum(self.natural_z(got))

    def sum_mp_rows(self, value):
        size = value.shape[0] // self.mn
        parts = [
            lax.dynamic_slice_in_dim(value, ((self.z + t) % self.mn) * size, size, 0).astype(BF)
            for t in range(self.mn)
        ]
        got = yield from self.direct(parts)
        total = sum(part.astype(F32) for part in got).astype(BF)
        got = yield from self.direct([total] * self.mn)
        return self.natural_rows(got)

    def sum_all(self, value):
        for bit in [1] + self.chips:
            (got,) = yield [(bit, 0, value)]
            value = value + got
        return (yield from self.sum_mp(value))

    def sum_all_rows(self, value):
        for b in range(self.bits):
            half = value.shape[0] // 2
            low, high = value[:half], value[half:]
            up = (self.d >> b) & 1
            give = jnp.where(up == 1, low, high).astype(BF)
            (got,) = yield [(1 << b, 0, give)]
            value = jnp.where(up == 1, high, low) + got.astype(F32)
        value = value.astype(BF)
        value = yield from self.direct([value] * self.mn)
        size = value[0].shape[0]
        value = self.natural_rows(value).astype(F32)
        value = sum(value[k * size : (k + 1) * size] for k in range(self.mn)).astype(BF)
        for b in reversed(range(self.bits)):
            (other,) = yield [(1 << b, 0, value)]
            up = (self.d >> b) & 1
            value = jnp.concatenate(
                [jnp.where(up == 1, other, value), jnp.where(up == 1, value, other)], 0
            )
        return value


def heads_of(value):
    return value.reshape(value.shape[0], -1, HEAD)


def per_device(
    dn,
    mn,
    bytes_in,
    mask_ratio,
    mask_starts,
    mask_lengths,
    latents,
    col,
    attn_out,
    mlp_down,
    enc_kv,
    dec_kv,
    dec_queries,
    dec_square,
    vocab,
    gains,
    mask_vec,
    byte_gain,
    cotangent,
):
    links = Links(dn, mn)
    d, z = links.d, links.z
    items, rows, wide_in = bytes_in.shape
    repeat = mn // items
    assert repeat * items == mn
    seq = rows * mn
    mine = z % items
    chan = col.shape[1] * dn
    enc_scale = chan ** (-0.5)
    dec_scale = wide_in ** (-0.5)

    n_gain, own_gain = gains.shape
    own_in = mask_vec.shape[0]
    in_rows = enc_kv.shape[1]
    col_rows, col_wide = col.shape[1:]
    own_lat, lat_cols = latents.shape
    small = jnp.concatenate([gains.reshape(-1), mask_vec, byte_gain])
    n_small = small.shape[0]
    line = jnp.pad(small, (0, -n_small % lat_cols)).reshape(-1, lat_cols)
    line = jnp.pad(line, ((0, -line.shape[0] % max(16 // mn, 1)), (0, 0)))
    chips = links.chips

    def head_task():
        early = yield from links.direct([jnp.concatenate([latents, line], 0)] * mn)
        early = links.natural_z(early)
        lat = [part[:own_lat] for part in early]
        tall = jnp.concatenate([part[own_lat:] for part in early] + lat, 0)
        n_line = tall.shape[0] - own_lat * mn
        heavy = jnp.concatenate([col[0], enc_kv[0]], 0)
        heavy = jnp.pad(heavy, ((n_line, own_lat * mn - heavy.shape[0]), (0, 0)))
        return (yield from links.spread(jnp.concatenate([tall, heavy], 1), chips))

    cat = lambda parts: jnp.concatenate(parts, -1)

    own_sq = dec_square.shape[1]
    n_voc = vocab.shape[1]
    deck_wide = dec_kv.shape[2]
    own_query, own_pos = dec_queries.T.shape

    def gathered(parts, wide):
        parts = [jnp.pad(p, ((0, -p.shape[0] % 16), (0, wide - p.shape[1]))) for p in parts]
        whole = jnp.concatenate(parts, 0)
        tall = whole.shape[0]
        whole = lax.all_gather(whole, ("dp", "mp"), axis=0, tiled=True)
        whole = whole.reshape(dn, mn, tall, wide)
        edges = [0]
        for p in parts:
            edges.append(edges[-1] + p.shape[0])
        return whole, edges

    def beside(got, row, col, size, wide):
        parts = [got[:, m, row : row + size, col : col + wide] for m in range(mn)]
        return jnp.concatenate([part.reshape(dn * size, wide) for part in parts], 1)

    side = lambda *parts: jnp.concatenate(parts, 1)
    w_one, at_one = gathered(
        [
            side(attn_out[0], col[1]),
            side(mlp_down[0], col[2]),
            side(col[3], col[4]),
            side(attn_out[1], jnp.pad(enc_kv[1], ((0, col_rows - in_rows), (0, 0)))),
        ],
        2 * col_wide,
    )
    late_wide = 2 * (col_wide + deck_wide)
    sq = side(dec_square[0], dec_square[1], vocab)
    sq = jnp.pad(sq, ((0, -own_sq % 16), (0, -sq.shape[1] % late_wide)))
    halves = 2 if own_query % 32 == 0 and 2 * own_pos <= late_wide else 1
    part_rows = own_query // halves
    def first_weight(k):
        return beside(w_one, at_one[k // 2], (k % 2) * col_wide, col_rows, col_wide)

    def last_weights():
        edge = 0
        out = []
        for wide in (col_wide, col_wide, deck_wide, deck_wide):
            out.append(beside(w_two, 0, edge, col_rows, wide))
            edge += wide
        query = [
            w_two[:, :, at_two[1] : at_two[1] + part_rows, h * own_pos : (h + 1) * own_pos]
            for h in range(halves)
        ]
        query = jnp.stack(query, 1).transpose(0, 1, 3, 2, 4).reshape(dn * own_query, seq)
        lines = jnp.concatenate(
            [w_two[:, :, row : row + own_sq] for row in at_two[2:-1]], -1
        ).reshape(dn * mn * own_sq, -1)
        return out + [
            query,
            lines[:, :wide_in],
            lines[:, wide_in : 2 * wide_in],
            lines[:, 2 * wide_in : 2 * wide_in + n_voc],
        ]

    steps = jnp.arange(rows, dtype=jnp.int32)
    masked = jax.vmap(lambda a, b, c: masked_rows(a, b, c, z * rows + steps))(
        mask_ratio, mask_starts, mask_lengths
    )[:, :, None]
    masked_item = masked_rows(
        mask_ratio[mine], mask_starts[mine], mask_lengths[mine], jnp.arange(seq, dtype=jnp.int32)
    )
    cot = cotangent.swapaxes(1, 2)
    head = links.free(head_task())
    held = links.by_index(jnp.stack([head[r] for r in range(dn)]))

    late_parts = [
        side(col[5], mlp_down[1], dec_kv[0], dec_kv[1]),
        jnp.concatenate(jnp.split(dec_queries.T, halves, 0), 1),
    ] + jnp.split(sq, sq.shape[1] // late_wide, 1)
    n_lat = own_lat * mn
    n_line = line.shape[0] * mn
    smalls = held[:, :n_line, :lat_cols].reshape(dn, mn, -1)[:, :, :n_small].astype(F32)
    gain = smalls[:, :, : n_gain * own_gain].reshape(dn, mn, n_gain, own_gain)
    gain = gain.transpose(2, 0, 1, 3).reshape(n_gain, -1)
    vecs = smalls[:, :, n_gain * own_gain :]
    mask_all = vecs[:, :, :own_in].reshape(-1)
    byte_gain_all = vecs[:, :, own_in:].reshape(-1)
    lat = held[:, n_line:, :lat_cols].transpose(1, 0, 2).reshape(n_lat, -1).astype(F32)
    col_zero = held[:, n_line : n_line + col_rows, lat_cols:].reshape(dn * col_rows, -1)
    key_w = held[:, n_line + col_rows : n_line + col_rows + in_rows, lat_cols:]
    key_w = key_w.reshape(dn * in_rows, -1)
    lat_norm = layer_norm(lat, gain[0]).astype(BF)
    query_m = (dot(lat_norm, col_zero) * enc_scale).astype(BF)
    query_key = dot_t(query_m, key_w)
    query_key = links.free(links.sum_mp_rows(query_key))

    raw = bytes_in.astype(F32)
    start = raw + masked * (mask_all - raw)
    byte_norm = layer_norm(start, byte_gain_all).astype(BF)

    scores = jnp.einsum("ld,ird->ilr", query_key, byte_norm, preferred_element_type=F32)
    top = jnp.max(scores, -1)
    weights = jnp.exp(scores - top[:, :, None])
    below = jnp.sum(weights, -1)
    mix = jnp.einsum("ilr,ird->ild", weights.astype(BF), byte_norm, preferred_element_type=F32)
    mix = mix.astype(BF)

    def mix_task(mix, top, below):
        block = lambda t: lax.dynamic_index_in_dim(mix, links.z_of(t) % items, 0, False)
        pack = jnp.stack([top, below])
        got = yield [("z", t, pack) for t in range(1, mn)] + [("z", 1, block(1))]
        stats = jnp.stack([pack] + list(got[: mn - 1]))
        top_all = jnp.max(stats[:, 0], 0)
        shares = jnp.exp(stats[:, 0] - top_all)
        total = sum(links.natural_z(list(stats[:, 1] * shares)))
        pick = lambda t, i: lax.dynamic_index_in_dim(shares[t], i % items, 0, False)[:, None]
        arrived = got[-1].astype(F32) * pick(1 % mn, links.z_of(2))
        for t in range(2, mn):
            arrived = (arrived + block(t).astype(F32) * pick(0, links.z_of(t))).astype(BF)
            (arrived,) = yield [("z", 1, arrived)]
            arrived = arrived.astype(F32)
        whole = arrived + block(0).astype(F32) * pick(0, z)
        whole = whole / lax.dynamic_index_in_dim(total, mine, 0, False)[:, None]
        return whole.astype(BF), shares[0] / total

    assert mn > 2
    mix, share = links.free(mix_task(mix, top, below))
    w_out0, w_up0, w_down0, w_q, w_k, w_v, w_out1 = (first_weight(k) for k in range(7))
    w_value = beside(w_one, at_one[3], col_wide, in_rows, col_wide)
    late_parts[0] = late_parts[0] + (nothing_of(w_one[0, 0]) + nothing_of(mix)).astype(BF)
    w_two, at_two = gathered(
        late_parts,
        late_wide,
    )


    def cot_task():
        held = cot + nothing_of(w_two[0, 0]).astype(BF)
        parts = [lax.dynamic_index_in_dim(held, (z + t) % mn % items, 0, False) for t in range(mn)]
        parts = yield from links.direct(parts)
        return (links.natural_columns(parts).astype(F32) * (masked_item / repeat)[None, :]).astype(BF)

    attended = dot(mix, w_value).astype(BF)
    first = lat + dot_t(attended, w_out0)
    norm1 = layer_norm(first, gain[1]).astype(BF)
    hidden1 = dot(norm1, w_up0)
    active1 = gelu_exact(hidden1).astype(BF)
    second = first + dot_t(active1, w_down0)
    norm2 = layer_norm(second, gain[2]).astype(BF)
    query = heads_of((dot(norm2, w_q) * HEAD ** (-0.5)).astype(BF))
    keys = heads_of(dot(norm2, w_k).astype(BF))
    values = heads_of(dot(norm2, w_v).astype(BF))
    s = jnp.einsum("qhe,khe->hqk", query, keys, preferred_element_type=F32)
    probs = jnp.exp(s - jnp.max(s, -1, keepdims=True))
    probs = probs / jnp.sum(probs, -1, keepdims=True)
    mixed = jnp.einsum("hqk,khe->qhe", probs.astype(BF), values, preferred_element_type=F32)
    mixed = mixed.astype(BF).reshape(n_lat, -1)
    third = second + dot_t(mixed, w_out1)
    norm3 = layer_norm(third, gain[3]).astype(BF)
    w_up1, w_down1, w_dk, w_dv, x_query, w_dq, w_do, w_voc = last_weights()
    hidden3 = dot(norm3, w_up1)
    active3 = gelu_exact(hidden3).astype(BF)
    fourth = third + dot_t(active3, w_down1)
    norm4 = layer_norm(fourth, gain[4]).astype(BF)
    grad_logits = links.free(cot_task())

    dec_keys = dot(norm4, w_dk).astype(BF)
    dec_values = dot(norm4, w_dv).astype(BF)
    key_query = (dot_t(dec_keys, w_dq) * dec_scale).astype(BF)
    value_out = dot(dec_values, w_do).astype(BF)
    value_voc = dot(value_out, w_voc).astype(BF)
    s = dot(key_query, x_query)
    p = jnp.exp(s - jnp.max(s, 0, keepdims=True))
    p = p / jnp.sum(p, 0, keepdims=True)
    p_low = p.astype(BF)
    logits_t = dot_tn(value_voc, p_low).astype(BF)
    d_p = dot(value_voc, grad_logits)
    d_s = (p * (d_p - jnp.sum(d_p * p, 0, keepdims=True))).astype(BF)
    d_vv = dot_t(p_low, grad_logits).astype(BF)
    d_kq = (dot_t(d_s, x_query) * dec_scale).astype(BF)
    d_vo = dot_t(d_vv, w_voc).astype(BF)
    d_dk = dot(d_kq, w_dq).astype(BF)
    d_dv = dot_t(d_vo, w_do).astype(BF)

    def logits_task():
        part = lambda t: lax.dynamic_slice_in_dim(logits_t, links.z_of(t) * rows, rows, 1)
        own = part(0)
        got = yield [("z", mn - t, part(t)) for t in range(1, items)]
        out = jnp.concatenate(([own] + list(got)) * 2, 1)
        first = ((items - mine) % items) * rows
        out = lax.dynamic_slice_in_dim(out, first, items * rows, 1)
        return out.reshape(-1, items, rows).transpose(1, 2, 0)

    def by_columns(value, t):
        size = value.shape[-1] // mn
        return lax.slice_in_dim(value, t * size, (t + 1) * size, axis=value.ndim - 1)

    def by_own_columns(value, t):
        size = value.shape[-1] // mn
        return lax.dynamic_slice_in_dim(value, links.z_of(t) * size, size, value.ndim - 1)

    def by_own_rows(value, t):
        size = value.shape[-2] // mn
        return lax.dynamic_slice_in_dim(value, links.z_of(t) * size, size, value.ndim - 2)

    def summed(*terms):
        whole = jnp.concatenate([term.astype(BF) for term in terms], 1)
        ready = nothing_of(whole)
        whole = lax.psum_scatter(whole, "dp", scatter_dimension=0, tiled=True)
        edge, out = 0, []
        for term in terms:
            out.append(whole[:, edge : edge + term.shape[1]])
            edge += term.shape[1]
        return ready, out

    def last_columns(terms):
        return links.free(
            links.sum_split(lambda t: jnp.concatenate([by_own_columns(v, t) for v in terms], 1))
        )

    def columns(terms):
        return links.free(
            links.sum_ring(lambda t: jnp.concatenate([by_own_columns(v, t) for v in terms], 1))
        )

    d_res, d_gain4 = norm_back(fourth, gain[4], dot_t(d_dk, w_dk) + dot_t(d_dv, w_dv))
    d_gain4 = jnp.sum(d_gain4, 0)
    ready, rows_a = summed(
        dot_tn(key_query, d_s),
        dot_tn(d_kq, dec_keys),
        dot_tn(dec_values, d_vo),
        dot_tn(value_out, d_vv),
    )
    d_res = d_res + ready
    g_deck = [dot_tn(norm4, d_dk), dot_tn(norm4, d_dv)]

    def ffn_back(d_res, resid, gain, w_up, w_down, normed, hidden, active):
        branch = d_res.astype(BF)
        d_hidden = (dot(branch, w_down) * gelu_slope(hidden)).astype(BF)
        grads = [dot_tn(normed, d_hidden), dot_tn(branch, active)]
        extra, d_gain = norm_back(resid, gain, dot_t(d_hidden, w_up))
        return d_res + extra, jnp.sum(d_gain, 0), grads

    d_res, d_gain3, g_ffn1 = ffn_back(
        d_res, third, gain[3], w_up1, w_down1, norm3, hidden3, active3
    )

    branch = d_res.astype(BF)
    d_mixed = heads_of(dot(branch, w_out1).astype(BF))
    d_probs = jnp.einsum("qhe,khe->hqk", d_mixed, values, preferred_element_type=F32)
    d_s = (probs * (d_probs - jnp.sum(d_probs * probs, -1, keepdims=True))).astype(BF)
    d_values = jnp.einsum("hqk,qhe->khe", probs.astype(BF), d_mixed, preferred_element_type=F32)
    d_keys = jnp.einsum("hqk,qhe->khe", d_s, query, preferred_element_type=F32)
    d_query = jnp.einsum("hqk,khe->qhe", d_s, keys, preferred_element_type=F32)
    d_values = d_values.astype(BF).reshape(n_lat, -1)
    d_keys = d_keys.astype(BF).reshape(n_lat, -1)
    d_query = (d_query * HEAD ** (-0.5)).astype(BF).reshape(n_lat, -1)
    ready, rows_b = summed(
        *g_deck,
        *g_ffn1,
        dot_tn(norm2, d_values),
        dot_tn(branch, mixed),
        dot_tn(norm2, d_query),
        dot_tn(norm2, d_keys),
    )
    extra, d_gain2 = norm_back(
        second, gain[2], dot_t(d_query, w_q) + dot_t(d_keys, w_k) + dot_t(d_values, w_v)
    )
    d_res, d_gain2 = d_res + extra + ready, jnp.sum(d_gain2, 0)
    d_res, d_gain1, g_ffn0 = ffn_back(
        d_res, first, gain[1], w_up0, w_down0, norm1, hidden1, active1
    )

    branch = d_res.astype(BF)
    d_attended = dot(branch, w_out0).astype(BF)
    mix_grad = dot_t(d_attended, w_value)
    value_term = dot_tn(mix, d_attended).astype(BF).reshape(dn, in_rows, chan)
    value_term = jnp.pad(value_term, ((0, 0), (0, col_rows - in_rows), (0, 0)))
    value_term = value_term.reshape(dn * col_rows, chan)
    ready, rows_c = summed(*g_ffn0, dot_tn(branch, attended), value_term)
    around = links.free(links.direct([(mix_grad * repeat + ready).astype(BF)] * mn))

    def latents_task():
        value = yield from links.sum_ring(lambda t: by_own_rows(branch, t))
        for bit in chips[::-1] + [1]:
            half = value.shape[1] // 2
            low, high = value[:, :half], value[:, half:]
            up = (d & bit) != 0
            (got,) = yield [(bit, 0, jnp.where(up, low, high).astype(BF))]
            value = jnp.where(up, high, low) + got.astype(F32)
        return value

    g_lat = links.free(latents_task())

    e_all = links.natural_rows(around).reshape(mn, n_lat, -1)[:items]
    norm_probs = weights * share[:, :, None]
    d_probs = jnp.einsum("ild,ird->ilr", e_all, byte_norm, preferred_element_type=F32)
    delta = jnp.sum(norm_probs * d_probs, -1)
    delta = links.free(links.sum_mp(delta))
    d_scores = (norm_probs * (d_probs - delta[:, :, None])).astype(BF)
    d_qk = jnp.einsum("ilr,ird->ld", d_scores, byte_norm, preferred_element_type=F32)
    d_qk = links.free(links.sum_all_rows(d_qk))
    d_bn = jnp.einsum("ilr,ld->ird", d_scores, query_key, preferred_element_type=F32)
    d_bn = d_bn + jnp.einsum(
        "ilr,ild->ird", norm_probs.astype(BF), e_all, preferred_element_type=F32
    )
    d_start, d_byte_gain = norm_back(start, byte_gain_all, d_bn)
    d_bytes = d_start * (1.0 - masked)
    d_mask = jnp.sum(d_start * masked, (0, 1))
    d_byte_gain = jnp.sum(d_byte_gain, (0, 1))
    logits = links.free(logits_task())

    d_query_m = (dot(d_qk, key_w) * enc_scale).astype(BF)
    d_lat_norm = links.free(
        links.sum_ring(
            lambda t, value=dot_t(d_query_m, col_zero).astype(BF): by_own_rows(value, t)
        )
    )
    d_qk_own = lax.dynamic_index_in_dim(d_qk.reshape(n_lat, dn, in_rows), d, 1, False)
    g_key = dot_tn(d_qk_own, query_m)
    lat_mine = lax.dynamic_slice_in_dim(lat_norm, d * col_rows, col_rows, 1)
    g_col0 = dot_tn(lat_mine, d_query_m)
    lat_own = lax.dynamic_slice_in_dim(lat, z * own_lat, own_lat, 0)
    d_lat, d_gain0 = norm_back(lat_own, gain[0], d_lat_norm)

    d_gains = jnp.stack([jnp.sum(d_gain0, 0) / dn, d_gain1, d_gain2, d_gain3, d_gain4])
    sums = jnp.concatenate([d_gains.reshape(-1), d_mask, d_byte_gain]).reshape(-1, 128)
    sums = links.free(links.sum_all(sums)).reshape(-1)
    place = d * mn + z
    g_gains = lax.dynamic_slice_in_dim(
        sums[: n_gain * chan].reshape(n_gain, chan), place * own_gain, own_gain, 1
    )
    g_mask = lax.dynamic_slice_in_dim(sums, n_gain * chan + place * own_in, own_in, 0)
    g_byte_gain = lax.dynamic_slice_in_dim(
        sums, n_gain * chan + wide_in + place * own_in, own_in, 0
    )
    g_lat = g_lat + lax.dynamic_slice_in_dim(d_lat, d * lat_cols, lat_cols, 1)
    split = lambda value, *wides: jnp.split(value, [sum(wides[: i + 1]) for i in range(len(wides) - 1)], 1)

    def rows_task(terms):
        value = jnp.concatenate(terms, 1)
        return links.sum_ring(lambda t: by_own_rows(value, t))

    g_xq, g_dq, g_do, g_voc = rows_a
    g_xq = columns([g_xq])
    g_sq = links.free(rows_task([g_dq, g_do, g_voc]))
    after = (nothing_of(g_sq) + nothing_of(g_xq)).astype(BF)
    g_b = columns([term + after for term in rows_b])
    g_dk, g_dv, g_up1, g_down1, g_v, g_out1, g_q, g_k = split(
        g_b, *([deck_wide] * 2 + [col_wide] * 6)
    )
    after = nothing_of(g_b).astype(BF)
    g_up0, g_down0, g_out0, g_value = split(last_columns([term + after for term in rows_c]), *[col_wide] * 4)
    g_value = g_value[:in_rows]
    return (
        logits,
        d_bytes,
        g_lat,
        jnp.stack([g_col0, g_up0, g_q, g_k, g_v, g_up1]),
        jnp.stack([g_out0, g_out1]),
        jnp.stack([g_down0, g_down1]),
        jnp.stack([g_key, g_value]),
        jnp.stack([g_dk, g_dv]),
        g_xq.T,
        jnp.stack([g_sq[:, :wide_in], g_sq[:, wide_in : 2 * wide_in]]),
        g_sq[:, 2 * wide_in :],
        g_gains,
        g_mask,
        g_byte_gain,
    )


def solution(mesh):
    return jax.shard_map(
        functools.partial(per_device, mesh.shape["dp"], mesh.shape["mp"]),
        mesh=mesh,
        in_specs=(
            P("dp", "mp", None),
            P("dp"),
            P("dp", None),
            P("dp", None),
            P("mp", "dp"),
            P(None, "dp", "mp"),
            P(None, "dp", "mp"),
            P(None, "dp", "mp"),
            P(None, "dp", "mp"),
            P(None, "dp", "mp"),
            P("mp", "dp"),
            P(None, ("dp", "mp"), None),
            P(("dp", "mp"), None),
            P(None, ("dp", "mp")),
            P(("dp", "mp")),
            P(("dp", "mp")),
            P("dp", "mp", None),
        ),
        out_specs=(
            P("dp", "mp", None),
            P("dp", "mp", None),
            P("mp", "dp"),
            P(None, "dp", "mp"),
            P(None, "dp", "mp"),
            P(None, "dp", "mp"),
            P(None, "dp", "mp"),
            P(None, "dp", "mp"),
            P("mp", "dp"),
            P(None, ("dp", "mp"), None),
            P(("dp", "mp"), None),
            P(None, ("dp", "mp")),
            P(("dp", "mp")),
            P(("dp", "mp")),
        ),
        check_vma=False,
    )
```

```python
import functools
import math

import jax
import jax.numpy as jnp
from jax import lax
from jax.sharding import PartitionSpec as P

HEAD = 160
BF = jnp.bfloat16
F32 = jnp.float32


def dot(left, right):
    return jnp.dot(left, right, preferred_element_type=F32)


def dot_t(left, right):
    return lax.dot_general(
        left,
        right,
        (((left.ndim - 1,), (right.ndim - 1,)), ((), ())),
        preferred_element_type=F32,
    )


def dot_tn(left, right):
    return lax.dot_general(left, right, (((0,), (0,)), ((), ())), preferred_element_type=F32)


def layer_norm(value, gain):
    centre = value - jnp.mean(value, -1, keepdims=True)
    spread_sq = jnp.mean(centre * centre, -1, keepdims=True)
    return centre * lax.rsqrt(spread_sq + 1e-05) * gain


def norm_back(value, gain, grad):
    centre = value - jnp.mean(value, -1, keepdims=True)
    inv = lax.rsqrt(jnp.mean(centre * centre, -1, keepdims=True) + 1e-05)
    unit = centre * inv
    scaled = grad * gain
    d_value = inv * (
        scaled
        - jnp.mean(scaled, -1, keepdims=True)
        - unit * jnp.mean(scaled * unit, -1, keepdims=True)
    )
    return d_value, grad * unit


def masked_rows(ratio, starts, lengths, positions):
    spaced = positions * 73 % 100 < ratio
    within = (positions[:, None] >= starts[None, :]) & (
        positions[:, None] < starts[None, :] + lengths[None, :]
    )
    return jnp.where(spaced | jnp.any(within, axis=1), 1.0, 0.0).astype(F32)


def gelu_exact(value):
    return jax.nn.gelu(value, approximate=False)


def gelu_slope(value):
    return 0.5 * (1.0 + lax.erf(value * 0.7071067811865476)) + value * 0.3989422804014327 * jnp.exp(
        -0.5 * value * value
    )


def nothing_of(value):
    return value[0, 0].astype(F32) * 0.0


class Links:
    def __init__(self, dn, mn):
        self.dn, self.mn = dn, mn
        self.bits = dn.bit_length() - 1
        assert 1 << self.bits == dn and mn & (mn - 1) == 0
        self.chips = [1 << b for b in range(1, self.bits)]
        self.d = lax.axis_index("dp")
        self.z = lax.axis_index("mp")

    def z_of(self, t):
        return (self.z - t) % self.mn

    def ring(self, value):
        parts = [value]
        for _ in range(self.mn - 1):
            parts += yield [("z", 1, parts[-1])]
        return parts

    def direct(self, values):
        got = yield [("z", t, values[t]) for t in range(1, self.mn)]
        return [values[0]] + list(got)

    def natural_z(self, parts):
        shape = parts[0].shape
        size = math.prod(shape[:-1])
        around = [parts[(-k) % self.mn].reshape(size, shape[-1]) for k in range(self.mn)] * 2
        first = ((self.mn - self.z) % self.mn) * size
        whole = lax.dynamic_slice_in_dim(jnp.concatenate(around, 0), first, self.mn * size, 0)
        return [whole[k * size : (k + 1) * size].reshape(shape) for k in range(self.mn)]

    def natural_rows(self, parts):
        size = parts[0].shape[0]
        around = jnp.concatenate([parts[(-k) % self.mn] for k in range(self.mn)] * 2, 0)
        return lax.dynamic_slice_in_dim(
            around, ((self.mn - self.z) % self.mn) * size, self.mn * size, 0
        )

    def natural_columns(self, parts):
        size = parts[0].shape[1]
        around = jnp.concatenate([parts[(-k) % self.mn] for k in range(self.mn)] * 2, 1)
        return lax.dynamic_slice_in_dim(
            around, ((self.mn - self.z) % self.mn) * size, self.mn * size, 1
        )

    def free(self, steps):
        got = None
        while True:
            try:
                sends = steps.send(got)
            except StopIteration as end:
                return end.value
            got = [self.send(*send) for send in sends]

    def send(self, lane, move, value):
        if lane == "z":
            pairs = [(i, (i + move) % self.mn) for i in range(self.mn)]
            return lax.ppermute(value, "mp", pairs)
        return lax.ppermute(value, "dp", [(i, i ^ lane) for i in range(self.dn)])

    def by_index(self, value):
        value = value.reshape((2,) * self.bits + value.shape[1:])
        for axis in range(self.bits):
            up = (self.d >> (self.bits - 1 - axis)) & 1
            value = jnp.where(up == 1, jnp.flip(value, axis), value)
        return value.reshape((self.dn,) + value.shape[self.bits :])

    def spread(self, piece, turned):
        pieces = {0: piece}
        ready = []
        for bit in turned:
            for key in list(pieces):
                mates, ready = ready, []
                got = yield [(bit, 0, pieces[key])] + [(1, 0, pieces[k]) for k in mates]
                pieces[key ^ bit] = got[0]
                pieces.update({k ^ 1: v for k, v in zip(mates, got[1:])})
                ready = [key ^ bit] + ([0] if key == 0 and bit == turned[0] else [])
        got = yield [(1, 0, pieces[k]) for k in ready]
        pieces.update({k ^ 1: v for k, v in zip(ready, got)})
        return pieces

    def sum_ring(self, block):
        total = block(1).astype(BF)
        for t in range(2, self.mn):
            (got,) = yield [("z", 1, total)]
            total = (got.astype(F32) + block(t).astype(F32)).astype(BF)
        (got,) = yield [("z", 1, total)]
        return got.astype(F32) + block(0).astype(F32)

    def sum_split(self, block):
        got = yield [("z", t, block(self.mn - t).astype(BF)) for t in range(1, self.mn)]
        return block(0).astype(F32) + sum(part.astype(F32) for part in got)

    def sum_mp(self, value):
        got = yield from self.direct([value] * self.mn)
        return sum(self.natural_z(got))

    def sum_mp_rows(self, value):
        size = value.shape[0] // self.mn
        parts = [
            lax.dynamic_slice_in_dim(value, ((self.z + t) % self.mn) * size, size, 0).astype(BF)
            for t in range(self.mn)
        ]
        got = yield from self.direct(parts)
        total = sum(part.astype(F32) for part in got).astype(BF)
        got = yield from self.direct([total] * self.mn)
        return self.natural_rows(got)

    def sum_all(self, value):
        for bit in [1] + self.chips:
            (got,) = yield [(bit, 0, value)]
            value = value + got
        return (yield from self.sum_mp(value))

    def sum_all_rows(self, value):
        for b in range(self.bits):
            half = value.shape[0] // 2
            low, high = value[:half], value[half:]
            up = (self.d >> b) & 1
            give = jnp.where(up == 1, low, high).astype(BF)
            (got,) = yield [(1 << b, 0, give)]
            value = jnp.where(up == 1, high, low) + got.astype(F32)
        value = value.astype(BF)
        value = yield from self.direct([value] * self.mn)
        size = value[0].shape[0]
        value = self.natural_rows(value).astype(F32)
        value = sum(value[k * size : (k + 1) * size] for k in range(self.mn)).astype(BF)
        for b in reversed(range(self.bits)):
            (other,) = yield [(1 << b, 0, value)]
            up = (self.d >> b) & 1
            value = jnp.concatenate(
                [jnp.where(up == 1, other, value), jnp.where(up == 1, value, other)], 0
            )
        return value


def heads_of(value):
    return value.reshape(value.shape[0], -1, HEAD)


def per_device(
    dn,
    mn,
    bytes_in,
    mask_ratio,
    mask_starts,
    mask_lengths,
    latents,
    col,
    attn_out,
    mlp_down,
    enc_kv,
    dec_kv,
    dec_queries,
    dec_square,
    vocab,
    gains,
    mask_vec,
    byte_gain,
    cotangent,
):
    links = Links(dn, mn)
    d, z = links.d, links.z
    items, rows, wide_in = bytes_in.shape
    repeat = mn // items
    assert repeat * items == mn
    seq = rows * mn
    mine = z % items
    chan = col.shape[1] * dn
    enc_scale = chan ** (-0.5)
    dec_scale = wide_in ** (-0.5)

    n_gain, own_gain = gains.shape
    own_in = mask_vec.shape[0]
    in_rows = enc_kv.shape[1]
    col_rows, col_wide = col.shape[1:]
    own_lat, lat_cols = latents.shape
    small = jnp.concatenate([gains.reshape(-1), mask_vec, byte_gain])
    n_small = small.shape[0]
    line = jnp.pad(small, (0, -n_small % lat_cols)).reshape(-1, lat_cols)
    line = jnp.pad(line, ((0, -line.shape[0] % max(16 // mn, 1)), (0, 0)))
    chips = links.chips

    def head_task():
        early = yield from links.direct([jnp.concatenate([latents, line], 0)] * mn)
        early = links.natural_z(early)
        lat = [part[:own_lat] for part in early]
        tall = jnp.concatenate([part[own_lat:] for part in early] + lat, 0)
        n_line = tall.shape[0] - own_lat * mn
        heavy = jnp.concatenate([col[0], enc_kv[0]], 0)
        heavy = jnp.pad(heavy, ((n_line, own_lat * mn - heavy.shape[0]), (0, 0)))
        return (yield from links.spread(jnp.concatenate([tall, heavy], 1), chips))

    cat = lambda parts: jnp.concatenate(parts, -1)

    own_sq = dec_square.shape[1]
    n_voc = vocab.shape[1]
    deck_wide = dec_kv.shape[2]
    own_query, own_pos = dec_queries.T.shape

    def gathered(parts, wide):
        parts = [jnp.pad(p, ((0, -p.shape[0] % 16), (0, wide - p.shape[1]))) for p in parts]
        whole = jnp.concatenate(parts, 0)
        tall = whole.shape[0]
        whole = lax.all_gather(whole, ("dp", "mp"), axis=0, tiled=True)
        whole = whole.reshape(dn, mn, tall, wide)
        edges = [0]
        for p in parts:
            edges.append(edges[-1] + p.shape[0])
        return whole, edges

    def beside(got, row, col, size, wide):
        parts = [got[:, m, row : row + size, col : col + wide] for m in range(mn)]
        return jnp.concatenate([part.reshape(dn * size, wide) for part in parts], 1)

    side = lambda *parts: jnp.concatenate(parts, 1)
    w_one, at_one = gathered(
        [
            side(attn_out[0], col[1]),
            side(mlp_down[0], col[2]),
            side(col[3], col[4]),
            side(attn_out[1], jnp.pad(enc_kv[1], ((0, col_rows - in_rows), (0, 0)))),
        ],
        2 * col_wide,
    )
    late_wide = 2 * (col_wide + deck_wide)
    sq = side(dec_square[0], dec_square[1], vocab)
    sq = jnp.pad(sq, ((0, -own_sq % 16), (0, -sq.shape[1] % late_wide)))
    halves = 2 if own_query % 32 == 0 and 2 * own_pos <= late_wide else 1
    part_rows = own_query // halves
    def first_weight(k):
        return beside(w_one, at_one[k // 2], (k % 2) * col_wide, col_rows, col_wide)

    def last_weights():
        edge = 0
        out = []
        for wide in (col_wide, col_wide, deck_wide, deck_wide):
            out.append(beside(w_two, 0, edge, col_rows, wide))
            edge += wide
        query = [
            w_two[:, :, at_two[1] : at_two[1] + part_rows, h * own_pos : (h + 1) * own_pos]
            for h in range(halves)
        ]
        query = jnp.stack(query, 1).transpose(0, 1, 3, 2, 4).reshape(dn * own_query, seq)
        lines = jnp.concatenate(
            [w_two[:, :, row : row + own_sq] for row in at_two[2:-1]], -1
        ).reshape(dn * mn * own_sq, -1)
        return out + [
            query,
            lines[:, :wide_in],
            lines[:, wide_in : 2 * wide_in],
            lines[:, 2 * wide_in : 2 * wide_in + n_voc],
        ]

    steps = jnp.arange(rows, dtype=jnp.int32)
    masked = jax.vmap(lambda a, b, c: masked_rows(a, b, c, z * rows + steps))(
        mask_ratio, mask_starts, mask_lengths
    )[:, :, None]
    masked_item = masked_rows(
        mask_ratio[mine], mask_starts[mine], mask_lengths[mine], jnp.arange(seq, dtype=jnp.int32)
    )
    cot = cotangent.swapaxes(1, 2)
    head = links.free(head_task())
    held = links.by_index(jnp.stack([head[r] for r in range(dn)]))

    late_parts = [
        side(col[5], mlp_down[1], dec_kv[0], dec_kv[1]),
        jnp.concatenate(jnp.split(dec_queries.T, halves, 0), 1),
    ] + jnp.split(sq, sq.shape[1] // late_wide, 1)
    n_lat = own_lat * mn
    n_line = line.shape[0] * mn
    smalls = held[:, :n_line, :lat_cols].reshape(dn, mn, -1)[:, :, :n_small].astype(F32)
    gain = smalls[:, :, : n_gain * own_gain].reshape(dn, mn, n_gain, own_gain)
    gain = gain.transpose(2, 0, 1, 3).reshape(n_gain, -1)
    vecs = smalls[:, :, n_gain * own_gain :]
    mask_all = vecs[:, :, :own_in].reshape(-1)
    byte_gain_all = vecs[:, :, own_in:].reshape(-1)
    lat = held[:, n_line:, :lat_cols].transpose(1, 0, 2).reshape(n_lat, -1).astype(F32)
    col_zero = held[:, n_line : n_line + col_rows, lat_cols:].reshape(dn * col_rows, -1)
    key_w = held[:, n_line + col_rows : n_line + col_rows + in_rows, lat_cols:]
    key_w = key_w.reshape(dn * in_rows, -1)
    lat_norm = layer_norm(lat, gain[0]).astype(BF)
    query_m = (dot(lat_norm, col_zero) * enc_scale).astype(BF)
    query_key = dot_t(query_m, key_w)
    query_key = links.free(links.sum_mp_rows(query_key))

    raw = bytes_in.astype(F32)
    start = raw + masked * (mask_all - raw)
    byte_norm = layer_norm(start, byte_gain_all).astype(BF)

    scores = jnp.einsum("ld,ird->ilr", query_key, byte_norm, preferred_element_type=F32)
    top = jnp.max(scores, -1)
    weights = jnp.exp(scores - top[:, :, None])
    below = jnp.sum(weights, -1)
    mix = jnp.einsum("ilr,ird->ild", weights.astype(BF), byte_norm, preferred_element_type=F32)
    mix = mix.astype(BF)

    def mix_task(mix, top, below):
        block = lambda t: lax.dynamic_index_in_dim(mix, links.z_of(t) % items, 0, False)
        pack = jnp.stack([top, below])
        got = yield [("z", t, pack) for t in range(1, mn)] + [("z", 1, block(1))]
        stats = jnp.stack([pack] + list(got[: mn - 1]))
        top_all = jnp.max(stats[:, 0], 0)
        shares = jnp.exp(stats[:, 0] - top_all)
        total = sum(links.natural_z(list(stats[:, 1] * shares)))
        pick = lambda t, i: lax.dynamic_index_in_dim(shares[t], i % items, 0, False)[:, None]
        arrived = got[-1].astype(F32) * pick(1 % mn, links.z_of(2))
        for t in range(2, mn):
            arrived = (arrived + block(t).astype(F32) * pick(0, links.z_of(t))).astype(BF)
            (arrived,) = yield [("z", 1, arrived)]
            arrived = arrived.astype(F32)
        whole = arrived + block(0).astype(F32) * pick(0, z)
        whole = whole / lax.dynamic_index_in_dim(total, mine, 0, False)[:, None]
        return whole.astype(BF), shares[0] / total

    assert mn > 2
    mix, share = links.free(mix_task(mix, top, below))
    w_out0, w_up0, w_down0, w_q, w_k, w_v, w_out1 = (first_weight(k) for k in range(7))
    w_value = beside(w_one, at_one[3], col_wide, in_rows, col_wide)
    late_parts[0] = late_parts[0] + (nothing_of(w_one[0, 0]) + nothing_of(mix)).astype(BF)
    w_two, at_two = gathered(
        late_parts,
        late_wide,
    )


    def cot_task():
        held = cot + nothing_of(w_two[0, 0]).astype(BF)
        parts = [lax.dynamic_index_in_dim(held, (z + t) % mn % items, 0, False) for t in range(mn)]
        parts = yield from links.direct(parts)
        return (links.natural_columns(parts).astype(F32) * (masked_item / repeat)[None, :]).astype(BF)

    attended = dot(mix, w_value).astype(BF)
    first = lat + dot_t(attended, w_out0)
    norm1 = layer_norm(first, gain[1]).astype(BF)
    hidden1 = dot(norm1, w_up0)
    active1 = gelu_exact(hidden1).astype(BF)
    second = first + dot_t(active1, w_down0)
    norm2 = layer_norm(second, gain[2]).astype(BF)
    query = heads_of((dot(norm2, w_q) * HEAD ** (-0.5)).astype(BF))
    keys = heads_of(dot(norm2, w_k).astype(BF))
    values = heads_of(dot(norm2, w_v).astype(BF))
    s = jnp.einsum("qhe,khe->hqk", query, keys, preferred_element_type=F32)
    probs = jnp.exp(s - jnp.max(s, -1, keepdims=True))
    probs = probs / jnp.sum(probs, -1, keepdims=True)
    mixed = jnp.einsum("hqk,khe->qhe", probs.astype(BF), values, preferred_element_type=F32)
    mixed = mixed.astype(BF).reshape(n_lat, -1)
    third = second + dot_t(mixed, w_out1)
    norm3 = layer_norm(third, gain[3]).astype(BF)
    w_up1, w_down1, w_dk, w_dv, x_query, w_dq, w_do, w_voc = last_weights()
    hidden3 = dot(norm3, w_up1)
    active3 = gelu_exact(hidden3).astype(BF)
    fourth = third + dot_t(active3, w_down1)
    norm4 = layer_norm(fourth, gain[4]).astype(BF)
    grad_logits = links.free(cot_task())

    dec_keys = dot(norm4, w_dk).astype(BF)
    dec_values = dot(norm4, w_dv).astype(BF)
    key_query = (dot_t(dec_keys, w_dq) * dec_scale).astype(BF)
    value_out = dot(dec_values, w_do).astype(BF)
    value_voc = dot(value_out, w_voc).astype(BF)
    s = dot(key_query, x_query)
    p = jnp.exp(s - jnp.max(s, 0, keepdims=True))
    p = p / jnp.sum(p, 0, keepdims=True)
    p_low = p.astype(BF)
    logits_t = dot_tn(value_voc, p_low).astype(BF)
    d_p = dot(value_voc, grad_logits)
    d_s = (p * (d_p - jnp.sum(d_p * p, 0, keepdims=True))).astype(BF)
    d_vv = dot_t(p_low, grad_logits).astype(BF)
    d_kq = (dot_t(d_s, x_query) * dec_scale).astype(BF)
    d_vo = dot_t(d_vv, w_voc).astype(BF)
    d_dk = dot(d_kq, w_dq).astype(BF)
    d_dv = dot_t(d_vo, w_do).astype(BF)

    def logits_task():
        part = lambda t: lax.dynamic_slice_in_dim(logits_t, links.z_of(t) * rows, rows, 1)
        own = part(0)
        got = yield [("z", mn - t, part(t)) for t in range(1, items)]
        out = jnp.concatenate(([own] + list(got)) * 2, 1)
        first = ((items - mine) % items) * rows
        out = lax.dynamic_slice_in_dim(out, first, items * rows, 1)
        return out.reshape(-1, items, rows).transpose(1, 2, 0)

    def by_columns(value, t):
        size = value.shape[-1] // mn
        return lax.slice_in_dim(value, t * size, (t + 1) * size, axis=value.ndim - 1)

    def by_own_columns(value, t):
        size = value.shape[-1] // mn
        return lax.dynamic_slice_in_dim(value, links.z_of(t) * size, size, value.ndim - 1)

    def by_own_rows(value, t):
        size = value.shape[-2] // mn
        return lax.dynamic_slice_in_dim(value, links.z_of(t) * size, size, value.ndim - 2)

    def summed(*terms):
        whole = jnp.concatenate([term.astype(BF) for term in terms], 1)
        ready = nothing_of(whole)
        whole = lax.psum_scatter(whole, "dp", scatter_dimension=0, tiled=True)
        edge, out = 0, []
        for term in terms:
            out.append(whole[:, edge : edge + term.shape[1]])
            edge += term.shape[1]
        return ready, out

    def last_columns(terms):
        return links.free(
            links.sum_split(lambda t: jnp.concatenate([by_own_columns(v, t) for v in terms], 1))
        )

    def columns(terms):
        return links.free(
            links.sum_ring(lambda t: jnp.concatenate([by_own_columns(v, t) for v in terms], 1))
        )

    d_res, d_gain4 = norm_back(fourth, gain[4], dot_t(d_dk, w_dk) + dot_t(d_dv, w_dv))
    d_gain4 = jnp.sum(d_gain4, 0)
    ready, rows_a = summed(
        dot_tn(key_query, d_s),
        dot_tn(d_kq, dec_keys),
        dot_tn(dec_values, d_vo),
        dot_tn(value_out, d_vv),
    )
    d_res = d_res + ready
    g_deck = [dot_tn(norm4, d_dk), dot_tn(norm4, d_dv)]

    def ffn_back(d_res, resid, gain, w_up, w_down, normed, hidden, active):
        branch = d_res.astype(BF)
        d_hidden = (dot(branch, w_down) * gelu_slope(hidden)).astype(BF)
        grads = [dot_tn(normed, d_hidden), dot_tn(branch, active)]
        extra, d_gain = norm_back(resid, gain, dot_t(d_hidden, w_up))
        return d_res + extra, jnp.sum(d_gain, 0), grads

    d_res, d_gain3, g_ffn1 = ffn_back(
        d_res, third, gain[3], w_up1, w_down1, norm3, hidden3, active3
    )

    branch = d_res.astype(BF)
    d_mixed = heads_of(dot(branch, w_out1).astype(BF))
    d_probs = jnp.einsum("qhe,khe->hqk", d_mixed, values, preferred_element_type=F32)
    d_s = (probs * (d_probs - jnp.sum(d_probs * probs, -1, keepdims=True))).astype(BF)
    d_values = jnp.einsum("hqk,qhe->khe", probs.astype(BF), d_mixed, preferred_element_type=F32)
    d_keys = jnp.einsum("hqk,qhe->khe", d_s, query, preferred_element_type=F32)
    d_query = jnp.einsum("hqk,khe->qhe", d_s, keys, preferred_element_type=F32)
    d_values = d_values.astype(BF).reshape(n_lat, -1)
    d_keys = d_keys.astype(BF).reshape(n_lat, -1)
    d_query = (d_query * HEAD ** (-0.5)).astype(BF).reshape(n_lat, -1)
    ready, rows_b = summed(
        *g_deck,
        *g_ffn1,
        dot_tn(norm2, d_values),
        dot_tn(branch, mixed),
        dot_tn(norm2, d_query),
        dot_tn(norm2, d_keys),
    )
    extra, d_gain2 = norm_back(
        second, gain[2], dot_t(d_query, w_q) + dot_t(d_keys, w_k) + dot_t(d_values, w_v)
    )
    d_res, d_gain2 = d_res + extra + ready, jnp.sum(d_gain2, 0)
    d_res, d_gain1, g_ffn0 = ffn_back(
        d_res, first, gain[1], w_up0, w_down0, norm1, hidden1, active1
    )

    branch = d_res.astype(BF)
    d_attended = dot(branch, w_out0).astype(BF)
    mix_grad = dot_t(d_attended, w_value)
    value_term = dot_tn(mix, d_attended).astype(BF).reshape(dn, in_rows, chan)
    value_term = jnp.pad(value_term, ((0, 0), (0, col_rows - in_rows), (0, 0)))
    value_term = value_term.reshape(dn * col_rows, chan)
    ready, rows_c = summed(*g_ffn0, dot_tn(branch, attended), value_term)
    around = links.free(links.direct([(mix_grad * repeat + ready).astype(BF)] * mn))

    def latents_task():
        value = yield from links.sum_ring(lambda t: by_own_rows(branch, t))
        for bit in chips[::-1] + [1]:
            half = value.shape[1] // 2
            low, high = value[:, :half], value[:, half:]
            up = (d & bit) != 0
            (got,) = yield [(bit, 0, jnp.where(up, low, high).astype(BF))]
            value = jnp.where(up, high, low) + got.astype(F32)
        return value

    g_lat = links.free(latents_task())

    e_all = links.natural_rows(around).reshape(mn, n_lat, -1)[:items]
    norm_probs = weights * share[:, :, None]
    d_probs = jnp.einsum("ild,ird->ilr", e_all, byte_norm, preferred_element_type=F32)
    delta = jnp.sum(norm_probs * d_probs, -1)
    delta = links.free(links.sum_mp(delta))
    d_scores = (norm_probs * (d_probs - delta[:, :, None])).astype(BF)
    d_qk = jnp.einsum("ilr,ird->ld", d_scores, byte_norm, preferred_element_type=F32)
    d_qk = links.free(links.sum_all_rows(d_qk))
    d_bn = jnp.einsum("ilr,ld->ird", d_scores, query_key, preferred_element_type=F32)
    d_bn = d_bn + jnp.einsum(
        "ilr,ild->ird", norm_probs.astype(BF), e_all, preferred_element_type=F32
    )
    d_start, d_byte_gain = norm_back(start, byte_gain_all, d_bn)
    d_bytes = d_start * (1.0 - masked)
    d_mask = jnp.sum(d_start * masked, (0, 1))
    d_byte_gain = jnp.sum(d_byte_gain, (0, 1))
    logits = links.free(logits_task())

    d_query_m = (dot(d_qk, key_w) * enc_scale).astype(BF)
    d_lat_norm = links.free(
        links.sum_ring(
            lambda t, value=dot_t(d_query_m, col_zero).astype(BF): by_own_rows(value, t)
        )
    )
    d_qk_own = lax.dynamic_index_in_dim(d_qk.reshape(n_lat, dn, in_rows), d, 1, False)
    g_key = dot_tn(d_qk_own, query_m)
    lat_mine = lax.dynamic_slice_in_dim(lat_norm, d * col_rows, col_rows, 1)
    g_col0 = dot_tn(lat_mine, d_query_m)
    lat_own = lax.dynamic_slice_in_dim(lat, z * own_lat, own_lat, 0)
    d_lat, d_gain0 = norm_back(lat_own, gain[0], d_lat_norm)

    d_gains = jnp.stack([jnp.sum(d_gain0, 0) / dn, d_gain1, d_gain2, d_gain3, d_gain4])
    sums = jnp.concatenate([d_gains.reshape(-1), d_mask, d_byte_gain]).reshape(-1, 128)
    sums = links.free(links.sum_all(sums)).reshape(-1)
    place = d * mn + z
    g_gains = lax.dynamic_slice_in_dim(
        sums[: n_gain * chan].reshape(n_gain, chan), place * own_gain, own_gain, 1
    )
    g_mask = lax.dynamic_slice_in_dim(sums, n_gain * chan + place * own_in, own_in, 0)
    g_byte_gain = lax.dynamic_slice_in_dim(
        sums, n_gain * chan + wide_in + place * own_in, own_in, 0
    )
    g_lat = g_lat + lax.dynamic_slice_in_dim(d_lat, d * lat_cols, lat_cols, 1)
    split = lambda value, *wides: jnp.split(value, [sum(wides[: i + 1]) for i in range(len(wides) - 1)], 1)

    def rows_task(terms):
        value = jnp.concatenate(terms, 1)
        return links.sum_ring(lambda t: by_own_rows(value, t))

    g_xq, g_dq, g_do, g_voc = rows_a
    g_xq = last_columns([g_xq])
    g_sq = links.free(rows_task([g_dq, g_do, g_voc]))
    after = (nothing_of(g_sq) + nothing_of(g_xq)).astype(BF)
    g_b = columns([term + after for term in rows_b])
    g_dk, g_dv, g_up1, g_down1, g_v, g_out1, g_q, g_k = split(
        g_b, *([deck_wide] * 2 + [col_wide] * 6)
    )
    after = nothing_of(g_b).astype(BF)
    g_up0, g_down0, g_out0, g_value = split(last_columns([term + after for term in rows_c]), *[col_wide] * 4)
    g_value = g_value[:in_rows]
    return (
        logits,
        d_bytes,
        g_lat,
        jnp.stack([g_col0, g_up0, g_q, g_k, g_v, g_up1]),
        jnp.stack([g_out0, g_out1]),
        jnp.stack([g_down0, g_down1]),
        jnp.stack([g_key, g_value]),
        jnp.stack([g_dk, g_dv]),
        g_xq.T,
        jnp.stack([g_sq[:, :wide_in], g_sq[:, wide_in : 2 * wide_in]]),
        g_sq[:, 2 * wide_in :],
        g_gains,
        g_mask,
        g_byte_gain,
    )


def solution(mesh):
    return jax.shard_map(
        functools.partial(per_device, mesh.shape["dp"], mesh.shape["mp"]),
        mesh=mesh,
        in_specs=(
            P("dp", "mp", None),
            P("dp"),
            P("dp", None),
            P("dp", None),
            P("mp", "dp"),
            P(None, "dp", "mp"),
            P(None, "dp", "mp"),
            P(None, "dp", "mp"),
            P(None, "dp", "mp"),
            P(None, "dp", "mp"),
            P("mp", "dp"),
            P(None, ("dp", "mp"), None),
            P(("dp", "mp"), None),
            P(None, ("dp", "mp")),
            P(("dp", "mp")),
            P(("dp", "mp")),
            P("dp", "mp", None),
        ),
        out_specs=(
            P("dp", "mp", None),
            P("dp", "mp", None),
            P("mp", "dp"),
            P(None, "dp", "mp"),
            P(None, "dp", "mp"),
            P(None, "dp", "mp"),
            P(None, "dp", "mp"),
            P(None, "dp", "mp"),
            P("mp", "dp"),
            P(None, ("dp", "mp"), None),
            P(("dp", "mp"), None),
            P(None, ("dp", "mp")),
            P(("dp", "mp")),
            P(("dp", "mp")),
        ),
        check_vma=False,
    )
```
